32 devices in a mesh: shell: 8 (over z, x), atom: 4 (over y, core).
Axes of the slice: x: 2, y: 2, z: 4, core: 2. Of those that a mesh axis runs over, the one named last changes fastest.
Arguments:
- rho: float32 [32768], P('shell'), may hold values from 0.5 to 1.5
- task_point: int32 [8, 32, 256], P('shell', 'atom'), may hold values from 0 to 4095
- task_count: int32 [8, 32], P('shell', 'atom'), may hold values from 1 to 256
- radial_index: int32 [8, 32, 256], P('shell', 'atom'), may hold values from 0 to 126
- fraction: float32 [8, 32, 256], P('shell', 'atom'), may hold values from 0 to 1
- angular: bfloat16 [8, 32, 49, 256], P('shell', 'atom'), may hold values from -6 to 6
- green: float32 [7, 128, 128], replicated, may hold values from -0.02734375 to 0.02734375
Outputs:
- potential: float32 [32768], P(('shell', 'atom'))
The draws below stay inside these ranges and needn't reach their ends.
Inputs may be any that keep to these rules, and one draw needn't show every extreme that they name: Slots j with j >= task_count of their atom and batch are unused.
All inputs are finite; a program needn't handle non-finite values.
Results may differ from the reference program's by a relative error of at most 0.005.
Values may be sent and summed in bfloat16 or wider, within the bound.
A program may use at most 64 MiB of HBM per device.

```python
import math
import jax
import jax.numpy as jnp
import numpy as np
from jax import lax

LMAX = 6
LM = 49
R = 128
SLOTS = 256
PTS = 4096
ATOMS = 32
NPTS = 32768
N_SHELL = 8
N_ATOM = 4


def with_ends(drawn, stream_key, smallest, largest):
    spot = [jax.random.randint(jax.random.fold_in(stream_key, axis), (), 0, length) for axis, length in enumerate(drawn.shape)]
    longest = drawn.shape.index(max(drawn.shape))
    neighbour = spot[:longest] + [(spot[longest] + 1) % drawn.shape[longest]] + spot[longest + 1:]
    return drawn.at[tuple(spot)].set(smallest).at[tuple(neighbour)].set(largest)


def shard_levels(own_key, dims, shards, least, high):
    def one(axis_at, parts):
        heights = jax.random.uniform(jax.random.fold_in(jax.random.fold_in(own_key, 6), axis_at), (parts,), jnp.float32, least / len(shards), high / len(shards))
        return jnp.repeat(jnp.exp(heights), dims[axis_at] // parts).reshape((-1,) + (1,) * (len(dims) - axis_at - 1))

    factor_of = one(*shards[0])
    for cut in shards[1:]:
        factor_of = factor_of * one(*cut)
    return factor_of


def scatter_about(stream_key, extent, deviation, limit, cuts=(), held_as=jnp.bfloat16):
    result = jax.random.normal(stream_key, extent, jnp.float32) * deviation
    if len(cuts) > 0:
        result = shard_levels(stream_key, extent, cuts, -0.22, 0.18) * result
    return jnp.clip(result, min=-limit, max=limit).astype(held_as)


def setup_inputs(seed: int = 0) -> dict:
    streams_of = jax.random.split(jax.random.key(seed), 8)
    rho = jnp.clip(0.5 + 1.0 * jax.random.uniform(streams_of[0], (NPTS,), jnp.float32) ** shard_levels(streams_of[0], (NPTS,), ((0, 8),), -0.2, 0.2), 0.5, 1.5)
    task_point = with_ends(jax.random.randint(streams_of[1], (N_SHELL, ATOMS, SLOTS), 0, PTS), jax.random.fold_in(streams_of[1], 1), 0, PTS - 1).astype(jnp.int32)
    task_count = with_ends(jax.random.randint(streams_of[2], (N_SHELL, ATOMS), 1, SLOTS + 1), jax.random.fold_in(streams_of[2], 1), 1, SLOTS).astype(jnp.int32)
    radial_index = with_ends(jax.random.randint(streams_of[3], (N_SHELL, ATOMS, SLOTS), 0, R - 1), jax.random.fold_in(streams_of[3], 1), 0, (R - 1) - 1).astype(jnp.int32)
    fraction = jnp.clip(1.0 * jax.random.uniform(streams_of[4], (N_SHELL, ATOMS, SLOTS), jnp.float32) ** shard_levels(streams_of[4], (N_SHELL, ATOMS, SLOTS), ((0, 8), (1, 4)), -0.2, 0.2), 0.0, 1.0)
    angular = scatter_about(streams_of[5], (N_SHELL, ATOMS, LM, SLOTS), 1.0, 6.0, ((0, 8), (1, 4)))
    green = scatter_about(streams_of[6], (LMAX + 1, R, R), (12 * SLOTS * SLOTS * N_SHELL * N_SHELL * N_ATOM // PTS) ** -0.5, 0.02734375, (), jnp.float32)
    return {"rho": rho, "task_point": task_point, "task_count": task_count, "radial_index": radial_index, "fraction": fraction, "angular": angular, "green": green}


def degree_table():
    return np.array([int(math.isqrt(i)) for i in range(LM)], dtype=np.int32)

def radial_rows(radial_index, fraction):
    grid = jnp.arange(R, dtype=jnp.int32)
    lower = (grid == radial_index[..., None]).astype(jnp.float32) * (1.0 - fraction)[..., None]
    upper = (grid == radial_index[..., None] + 1).astype(jnp.float32) * fraction[..., None]
    return (lower + upper).astype(jnp.bfloat16)

def reference(rho, task_point, task_count, radial_index, fraction, angular, green):
    density = rho.reshape(N_SHELL, PTS)
    slot_ids = jnp.arange(SLOTS, dtype=jnp.int32)

    def batch_terms(batch):
        live = (slot_ids[None, :] < task_count[batch][:, None]).astype(jnp.float32)
        picked = density[batch][task_point[batch]] * live
        weighted = (angular[batch].astype(jnp.float32) * picked[:, None, :]).astype(jnp.bfloat16)
        rows = radial_rows(radial_index[batch], fraction[batch])
        return (live, weighted, rows)

    def accumulate(batch, total):
        live, weighted, rows = batch_terms(batch)
        return total + jnp.einsum('als,asr->alr', weighted.astype(jnp.float32), rows.astype(jnp.float32), precision=lax.Precision.HIGHEST)
    moments = lax.fori_loop(0, N_SHELL, accumulate, jnp.zeros((ATOMS, LM, R), jnp.float32))
    kernels = green[degree_table()]
    table = jnp.einsum('alq,lqr->alr', moments, kernels, precision=lax.Precision.HIGHEST).astype(jnp.bfloat16)

    def evaluate(batch):
        live, weighted, rows = batch_terms(batch)
        radial = jnp.einsum('alr,asr->als', table.astype(jnp.float32), rows.astype(jnp.float32), precision=lax.Precision.HIGHEST)
        values = lax.optimization_barrier(jnp.sum(angular[batch].astype(jnp.float32) * radial, axis=1)) * live
        return jnp.zeros((PTS,), jnp.float32).at[task_point[batch].reshape(-1)].add(values.reshape(-1))
    potential = lax.map(evaluate, jnp.arange(N_SHELL, dtype=jnp.int32))
    return potential.reshape(N_SHELL * PTS)
```

```python
import functools
import math

import jax
import jax.numpy as jnp
from jax import lax
from jax.experimental import pallas as pl
from jax.experimental.pallas import tpu as pltpu
from jax.sharding import PartitionSpec as P

MESH = pl.DeviceIdType.MESH
LANES = 128
NT = (((1,), (1,)), ((), ()))


def repeat(count, body):
    if count <= 16:
        for i in range(count):
            body(i)
    else:
        lax.fori_loop(0, count, lambda i, c: (body(i), c)[1], 0)


def split2(x):
    high = x.astype(jnp.bfloat16)
    low = (x - high.astype(jnp.float32)).astype(jnp.bfloat16)
    return high, low


def kernel(n_shell, n_atom, rho_h, pts_h, cnt_h, idx_h, frac_h, ang_h, green_h, out_ref,
           rho_v, pts_v, cnt_v, idx_v, frac_v, ang_v, green_v,
           live_v, low_v, high_v, onehot, meta_v, rmeta, rang, rows_v, gh_v, gl_v,
           moments, val_v, rval, part_v, rpart,
           local_sem, s_ang, r_ang, s_meta, r_meta, s_val, r_val, s_part, r_part):
    me, ma = lax.axis_index("shell"), lax.axis_index("atom")
    atoms, lm, slots = ang_v.shape
    lmp = rang.shape[1]
    body_rows = (lm // 16) * 16
    rest = lm - body_rows
    degrees, width = green_v.shape[0], green_v.shape[1]
    coarse = rho_v.shape[0]

    def load(i, src, dst):
        copy = pltpu.make_async_copy(src, dst, local_sem.at[i])
        copy.start()
        return copy

    c_ang = load(0, ang_h.at[0], ang_v)
    c_pts = load(1, pts_h.at[0], pts_v)
    c_rho = load(2, rho_h, rho_v)
    c_idx = load(3, idx_h.at[0], idx_v)
    c_cnt = load(4, cnt_h, cnt_v)
    c_frac = load(5, frac_h.at[0], frac_v)
    c_green = load(6, green_h, green_v)

    def shell_at(k):
        return lax.rem(me + k, n_shell)

    def atom_at(k):
        return lax.rem(ma + k, n_atom)

    def far_first(i):
        half = n_shell // 2
        step = (i + 1) // 2
        return half + step * (1 - 2 * (i % 2))

    barrier = pltpu.get_barrier_semaphore()
    repeat(n_shell - 1, lambda i: pl.semaphore_signal(
        barrier, inc=1, device_id=(shell_at(i + 1), ma), device_id_type=MESH))
    repeat(n_atom - 1, lambda i: pl.semaphore_signal(
        barrier, inc=1, device_id=(me, atom_at(i + 1)), device_id_type=MESH))
    pl.semaphore_wait(barrier, n_shell + n_atom - 2)

    def ang_copy(to, slot):
        return pltpu.make_async_remote_copy(
            src_ref=ang_v.at[to, pl.ds(0, body_rows)], dst_ref=rang.at[slot, pl.ds(0, body_rows)],
            send_sem=s_ang.at[to], recv_sem=r_ang.at[slot],
            device_id=(to, ma), device_id_type=MESH)

    def meta_copy(to, slot):
        return pltpu.make_async_remote_copy(
            src_ref=meta_v.at[to], dst_ref=rmeta.at[slot],
            send_sem=s_meta.at[to], recv_sem=r_meta.at[slot],
            device_id=(to, ma), device_id_type=MESH)

    def val_copy(to, slot):
        return pltpu.make_async_remote_copy(
            src_ref=val_v.at[to], dst_ref=rval.at[slot],
            send_sem=s_val.at[to], recv_sem=r_val.at[slot],
            device_id=(to, ma), device_id_type=MESH)

    def part_copy(to, slot):
        return pltpu.make_async_remote_copy(
            src_ref=part_v.at[to], dst_ref=rpart.at[slot],
            send_sem=s_part.at[to], recv_sem=r_part.at[slot],
            device_id=(me, to), device_id_type=MESH)

    c_ang.wait()

    def send_ang(i):
        ang_copy(shell_at(far_first(i)), me).start()

    repeat(n_shell - 1, send_ang)
    rang[me, 0:body_rows] = ang_v[me, 0:body_rows]

    c_pts.wait()
    c_rho.wait()
    c_idx.wait()
    c_cnt.wait()
    c_frac.wait()
    low_v[...] = pts_v[...] & (LANES - 1)
    high_v[...] = pts_v[...] >> (LANES.bit_length() - 1)
    count_row = jnp.broadcast_to(cnt_v[...].astype(jnp.float32), (atoms, atoms))
    diagonal = (lax.broadcasted_iota(jnp.int32, (atoms, atoms), 0)
                == lax.broadcasted_iota(jnp.int32, (atoms, atoms), 1))
    counts = jnp.sum(jnp.where(diagonal, count_row, 0.0), axis=1, keepdims=True)
    slot_ids = lax.broadcasted_iota(jnp.int32, (atoms, slots), 1).astype(jnp.float32)
    live_v[...] = jnp.where(slot_ids < counts, idx_v[...].astype(jnp.float32), -8.0)

    rho = rho_v[...]
    rho_1, left = rho.astype(jnp.bfloat16), rho
    left = left - rho_1.astype(jnp.float32)
    rho_2, rho_3 = split2(left)
    rho_parts = jnp.concatenate(
        [rho_1.astype(jnp.float32), rho_2.astype(jnp.float32), rho_3.astype(jnp.float32)],
        axis=0).astype(jnp.bfloat16)
    fine_ids = lax.broadcasted_iota(jnp.int32, (LANES, slots), 0)
    coarse_ids = lax.broadcasted_iota(jnp.int32, (coarse, slots), 0)

    def build_meta(a):
        hot = jnp.where(fine_ids == low_v[pl.ds(a, 1), :], 1.0, 0.0).astype(jnp.bfloat16)
        onehot[a] = hot
        found = jnp.dot(rho_parts, hot, preferred_element_type=jnp.float32)
        found = found[0:coarse] + found[coarse:2 * coarse] + found[2 * coarse:3 * coarse]
        here = coarse_ids == high_v[pl.ds(a, 1), :]
        meta_v[a, 0:1, :] = jnp.sum(jnp.where(here, found, 0.0), axis=0, keepdims=True)
        meta_v[a, 1:2, :] = live_v[pl.ds(a, 1), :]
        meta_v[a, 2:3, :] = frac_v[pl.ds(a, 1), :]
        for j in range(rest):
            meta_v[a, 3 + j:4 + j, :] = ang_v[a, body_rows + j:body_rows + j + 1, :].astype(jnp.float32)

    def send_meta(i):
        to = shell_at(far_first(i))
        build_meta(to)
        meta_copy(to, me).start()

    repeat(n_shell - 1, send_meta)
    build_meta(me)
    rmeta[me] = meta_v[me]

    c_green.wait()
    green = green_v[...].reshape(degrees * width, width)
    gh, gl = split2(green)
    gh_v[...] = gh
    gl_v[...] = gl

    moments[...] = jnp.zeros_like(moments)
    grid_ids = lax.broadcasted_iota(jnp.int32, (width, slots), 0).astype(jnp.float32)
    tail_ids = lax.broadcasted_iota(jnp.int32, (lmp - body_rows, slots), 0)

    def add_batch(s):
        index, fraction = rmeta[s, 1:2, :], rmeta[s, 2:3, :]
        offset = grid_ids - index
        rows = jnp.where(offset == 0.0, 1.0 - fraction, jnp.where(offset == 1.0, fraction, 0.0))
        rows = rows.astype(jnp.bfloat16)
        rows_v[s] = rows
        tail = jnp.zeros((lmp - body_rows, slots), jnp.float32)
        for j in range(rest):
            tail = jnp.where(tail_ids == j, rmeta[s, 3 + j:4 + j, :], tail)
        rang[s, body_rows:lmp] = tail.astype(jnp.bfloat16)
        weighted = (rang[s].astype(jnp.float32) * rmeta[s, 0:1, :]).astype(jnp.bfloat16)
        moments[...] += lax.dot_general(weighted, rows, NT, preferred_element_type=jnp.float32)

    def take_batch(i):
        s = lax.rem(me + n_shell - far_first(n_shell - 2 - i), n_shell)
        ang_copy(me, s).wait_recv()
        meta_copy(me, s).wait_recv()
        add_batch(s)

    add_batch(me)
    repeat(n_shell - 1, take_batch)

    mom = moments[...]
    mom_h, mom_l = split2(mom)
    both = jnp.concatenate([mom_h.astype(jnp.float32), mom_l.astype(jnp.float32)], axis=0)
    row_ids = lax.broadcasted_iota(jnp.int32, (2 * lmp, width), 0)
    row_ids = jnp.where(row_ids >= lmp, row_ids - lmp, row_ids)
    spread = jnp.concatenate(
        [jnp.where((row_ids >= l * l) & (row_ids < (l + 1) * (l + 1)), both, 0.0)
         for l in range(degrees)], axis=1).astype(jnp.bfloat16)
    first = jnp.dot(spread, gh_v[...], preferred_element_type=jnp.float32)
    second = jnp.dot(spread[0:lmp], gl_v[...], preferred_element_type=jnp.float32)
    table = (first[0:lmp] + first[lmp:] + second).astype(jnp.bfloat16)

    def evaluate(b, out, at):
        radial = jnp.dot(table, rows_v[b], preferred_element_type=jnp.float32)
        out[at] = jnp.sum(rang[b].astype(jnp.float32) * radial, axis=0, keepdims=True)

    def send_val(i):
        to = shell_at(far_first(i))
        evaluate(to, val_v, to)
        val_copy(to, me).start()

    repeat(n_shell - 1, send_val)
    evaluate(me, rval, me)

    def placed(a):
        spot = jnp.where(coarse_ids == high_v[pl.ds(a, 1), :], rval[a], 0.0)
        spot_h, spot_l = split2(spot)
        spots = jnp.concatenate(
            [spot_h.astype(jnp.float32), spot_l.astype(jnp.float32)], axis=0).astype(jnp.bfloat16)
        return lax.dot_general(spots, onehot[a], NT, preferred_element_type=jnp.float32)

    def terms_of(i, terms):
        s = lax.rem(me + n_shell - far_first(n_shell - 2 - i), n_shell)
        val_copy(me, s).wait_recv()
        return terms + placed(s)

    terms = placed(me)
    if n_shell <= 16:
        for i in range(n_shell - 1):
            terms = terms_of(i, terms)
    else:
        terms = lax.fori_loop(0, n_shell - 1, terms_of, terms)
    terms = terms[0:coarse] + terms[coarse:]
    share = coarse // n_atom
    for g in range(n_atom):
        part_v[g] = terms[g * share:(g + 1) * share]

    repeat(n_atom - 1, lambda i: part_copy(atom_at(i + 1), ma).start())
    rpart[ma] = part_v[ma]

    def take_part(i):
        part_copy(ma, atom_at(i + 1)).wait_recv()

    repeat(n_atom - 1, take_part)
    total = rpart[0]
    for g in range(1, n_atom):
        total = total + rpart[g]
    out_ref[...] = total

    def finish(i):
        to = shell_at(i + 1)
        ang_copy(to, me).wait_send()
        meta_copy(to, me).wait_send()
        val_copy(to, me).wait_send()

    repeat(n_shell - 1, finish)
    repeat(n_atom - 1, lambda i: part_copy(atom_at(i + 1), ma).wait_send())


def solution(mesh):
    n_shell, n_atom = mesh.shape["shell"], mesh.shape["atom"]

    def per_device(rho, task_point, task_count, radial_index, fraction, angular, green):
        _, atoms, lm, slots = angular.shape
        points = rho.shape[0]
        degrees, width, _ = green.shape
        assert atoms == n_shell and points % (LANES * n_atom) == 0
        assert degrees == math.isqrt(lm)
        coarse = points // LANES
        share = coarse // n_atom
        lmp = (lm // 16 + 1) * 16
        meta_rows = 3 + lm % 16
        f32, bf16, i32 = jnp.float32, jnp.bfloat16, jnp.int32
        vmem = pltpu.VMEM
        scratch = [
            vmem((coarse, LANES), f32),
            vmem((atoms, slots), i32),
            vmem((1, atoms), i32),
            vmem((atoms, slots), i32),
            vmem((atoms, slots), f32),
            vmem((atoms, lm, slots), bf16),
            vmem((degrees, width, width), f32),
            vmem((atoms, slots), f32),
            vmem((atoms, slots), i32),
            vmem((atoms, slots), i32),
            vmem((atoms, LANES, slots), bf16),
            vmem((atoms, meta_rows, slots), f32),
            vmem((n_shell, meta_rows, slots), f32),
            vmem((n_shell, lmp, slots), bf16),
            vmem((n_shell, width, slots), bf16),
            vmem((degrees * width, width), bf16),
            vmem((degrees * width, width), bf16),
            vmem((lmp, width), f32),
            vmem((n_shell, 1, slots), f32),
            vmem((n_shell, 1, slots), f32),
            vmem((n_atom, share, LANES), f32),
            vmem((n_atom, share, LANES), f32),
            pltpu.SemaphoreType.DMA((7,)),
        ] + [pltpu.SemaphoreType.DMA((n_shell,))] * 6 + [pltpu.SemaphoreType.DMA((n_atom,))] * 2
        out = pl.pallas_call(
            functools.partial(kernel, n_shell, n_atom),
            out_shape=jax.ShapeDtypeStruct((share, LANES), f32),
            in_specs=[pl.BlockSpec(memory_space=pl.ANY)] * 7,
            out_specs=pl.BlockSpec(memory_space=pltpu.VMEM),
            scratch_shapes=scratch,
            compiler_params=pltpu.CompilerParams(
                collective_id=0, has_side_effects=True, vmem_limit_bytes=48 * 1024 * 1024),
            name="hartree",
        )(rho.reshape(coarse, LANES), task_point, task_count, radial_index, fraction, angular, green)
        return out.reshape(share * LANES)

    in_specs = (
        P("shell"),
        P("shell", "atom", None),
        P("shell", "atom"),
        P("shell", "atom", None),
        P("shell", "atom", None),
        P("shell", "atom", None, None),
        P(),
    )
    return jax.shard_map(
        per_device, mesh=mesh, in_specs=in_specs, out_specs=P(("shell", "atom")), check_vma=False
    )
```

```python
import functools
import math

import jax
import jax.numpy as jnp
from jax import lax
from jax.experimental import pallas as pl
from jax.experimental.pallas import tpu as pltpu
from jax.sharding import PartitionSpec as P

MESH = pl.DeviceIdType.MESH
LANES = 128
NT = (((1,), (1,)), ((), ()))


def repeat(count, body):
    if count <= 16:
        for i in range(count):
            body(i)
    else:
        lax.fori_loop(0, count, lambda i, c: (body(i), c)[1], 0)


def accumulate(count, body, total):
    if count <= 16:
        for i in range(count):
            total = total + body(i)
        return total
    return lax.fori_loop(0, count, lambda i, c: c + body(i), total)


def split2(x):
    high = x.astype(jnp.bfloat16)
    low = (x - high.astype(jnp.float32)).astype(jnp.bfloat16)
    return high, low


def kernel(n_shell, n_atom, rho_h, pts_h, cnt_h, idx_h, frac_h, ang_h, green_h, out_ref,
           rho_v, pts_v, cnt_v, idx_v, frac_v, ang_s, ang_f, ang_v, green_v,
           live_v, low_v, high_v, onehot, meta_v, rmeta, rang, rows_v, gh_v, gl_v,
           val_v, rval, part_v, rpart,
           local_sem, s_ang, r_ang, s_meta, r_meta, s_val, r_val, s_part, r_part):
    me, ma = lax.axis_index("shell"), lax.axis_index("atom")
    lm, atoms, slots = ang_s.shape
    lmp = rang.shape[1]
    body_rows = ang_v.shape[1]
    rest = lm - body_rows
    halves = slots // LANES
    degrees, width = green_v.shape[0], green_v.shape[1]
    coarse = rho_v.shape[0]

    def load(i, src, dst):
        copy = pltpu.make_async_copy(src, dst, local_sem.at[i])
        copy.start()
        return copy

    c_ang = load(0, ang_h.at[0], ang_s)
    c_pts = load(1, pts_h.at[0], pts_v)
    c_rho = load(2, rho_h, rho_v)
    c_idx = load(3, idx_h.at[0], idx_v)
    c_cnt = load(4, cnt_h, cnt_v)
    c_frac = load(5, frac_h.at[0], frac_v)
    c_green = load(6, green_h, green_v)

    def shell_at(k):
        return lax.rem(me + k, n_shell)

    def atom_at(k):
        return lax.rem(ma + k, n_atom)

    def far_first(i):
        half = n_shell // 2
        step = (i + 1) // 2
        return half + step * (1 - 2 * (i % 2))

    barrier = pltpu.get_barrier_semaphore()
    repeat(n_shell - 1, lambda i: pl.semaphore_signal(
        barrier, inc=1, device_id=(shell_at(i + 1), ma), device_id_type=MESH))
    repeat(n_atom - 1, lambda i: pl.semaphore_signal(
        barrier, inc=1, device_id=(me, atom_at(i + 1)), device_id_type=MESH))

    def ang_copy(to, slot):
        return pltpu.make_async_remote_copy(
            src_ref=ang_v.at[to], dst_ref=rang.at[slot, pl.ds(0, body_rows)],
            send_sem=s_ang.at[to], recv_sem=r_ang.at[slot],
            device_id=(to, ma), device_id_type=MESH)

    def meta_copy(to, slot):
        return pltpu.make_async_remote_copy(
            src_ref=meta_v.at[to], dst_ref=rmeta.at[slot],
            send_sem=s_meta.at[to], recv_sem=r_meta.at[slot],
            device_id=(to, ma), device_id_type=MESH)

    def val_copy(to, slot):
        return pltpu.make_async_remote_copy(
            src_ref=val_v.at[to], dst_ref=rval.at[slot],
            send_sem=s_val.at[to], recv_sem=r_val.at[slot],
            device_id=(to, ma), device_id_type=MESH)

    def part_copy(to, slot):
        return pltpu.make_async_remote_copy(
            src_ref=part_v.at[to], dst_ref=rpart.at[slot],
            send_sem=s_part.at[to], recv_sem=r_part.at[slot],
            device_id=(me, to), device_id_type=MESH)

    c_ang.wait()

    def widen(m):
        at = pl.multiple_of(m * atoms, 8) if atoms % 8 == 0 else m * atoms
        for h in range(halves):
            ang_f[h, pl.ds(at, atoms), :] = ang_s[m, :, h * LANES:(h + 1) * LANES].astype(jnp.float32)

    def by_atom(a):
        for h in range(halves):
            ang_v[a, :, h * LANES:(h + 1) * LANES] = ang_f[
                h, pl.ds(a, body_rows, stride=atoms), :].astype(jnp.bfloat16)

    if atoms <= 16:
        for m in range(lm):
            widen(m)
    else:
        repeat(lm, widen)
    repeat(atoms, by_atom)
    pl.semaphore_wait(barrier, n_shell + n_atom - 2)
    repeat(n_shell - 1, lambda i: ang_copy(shell_at(far_first(i)), me).start())
    rang[me, 0:body_rows] = ang_v[me]

    c_pts.wait()
    c_rho.wait()
    c_idx.wait()
    c_cnt.wait()
    c_frac.wait()
    low_v[...] = pts_v[...] & (LANES - 1)
    high_v[...] = pts_v[...] >> (LANES.bit_length() - 1)
    count_row = jnp.broadcast_to(cnt_v[...].astype(jnp.float32), (atoms, atoms))
    diagonal = (lax.broadcasted_iota(jnp.int32, (atoms, atoms), 0)
                == lax.broadcasted_iota(jnp.int32, (atoms, atoms), 1))
    counts = jnp.sum(jnp.where(diagonal, count_row, 0.0), axis=1, keepdims=True)
    slot_ids = lax.broadcasted_iota(jnp.int32, (atoms, slots), 1).astype(jnp.float32)
    live_v[...] = jnp.where(slot_ids < counts, idx_v[...].astype(jnp.float32), -8.0)

    rho = rho_v[...]
    rho_1, left = rho.astype(jnp.bfloat16), rho
    left = left - rho_1.astype(jnp.float32)
    rho_2, rho_3 = split2(left)
    rho_parts = jnp.concatenate(
        [rho_1.astype(jnp.float32), rho_2.astype(jnp.float32), rho_3.astype(jnp.float32)],
        axis=0).astype(jnp.bfloat16)
    fine_ids = lax.broadcasted_iota(jnp.int32, (LANES, slots), 0)
    coarse_ids = lax.broadcasted_iota(jnp.int32, (coarse, slots), 0)

    def build_meta(a):
        hot = jnp.where(fine_ids == low_v[pl.ds(a, 1), :], 1.0, 0.0).astype(jnp.bfloat16)
        onehot[a] = hot
        found = jnp.dot(rho_parts, hot, preferred_element_type=jnp.float32)
        found = found[0:coarse] + found[coarse:2 * coarse] + found[2 * coarse:3 * coarse]
        here = coarse_ids == high_v[pl.ds(a, 1), :]
        meta_v[a, 0:1, :] = jnp.sum(jnp.where(here, found, 0.0), axis=0, keepdims=True)
        meta_v[a, 1:2, :] = live_v[pl.ds(a, 1), :]
        meta_v[a, 2:3, :] = frac_v[pl.ds(a, 1), :]
        for j in range(rest):
            for h in range(halves):
                meta_v[a, 3 + j:4 + j, h * LANES:(h + 1) * LANES] = ang_f[
                    h, pl.ds((body_rows + j) * atoms + a, 1), :]

    repeat(atoms, build_meta)
    repeat(n_shell - 1, lambda i: meta_copy(shell_at(far_first(i)), me).start())
    rmeta[me] = meta_v[me]

    c_green.wait()
    green = green_v[...].reshape(degrees * width, width)
    gh, gl = split2(green)
    gh_v[...] = gh
    gl_v[...] = gl

    grid_ids = lax.broadcasted_iota(jnp.int32, (width, slots), 0).astype(jnp.float32)
    tail_ids = lax.broadcasted_iota(jnp.int32, (lmp - body_rows, slots), 0)

    def add_batch(s):
        index, fraction = rmeta[s, 1:2, :], rmeta[s, 2:3, :]
        offset = grid_ids - index
        rows = jnp.where(offset == 0.0, 1.0 - fraction, jnp.where(offset == 1.0, fraction, 0.0))
        rows = rows.astype(jnp.bfloat16)
        rows_v[s] = rows
        tail = jnp.zeros((lmp - body_rows, slots), jnp.float32)
        for j in range(rest):
            tail = jnp.where(tail_ids == j, rmeta[s, 3 + j:4 + j, :], tail)
        rang[s, body_rows:lmp] = tail.astype(jnp.bfloat16)
        weighted = (rang[s].astype(jnp.float32) * rmeta[s, 0:1, :]).astype(jnp.bfloat16)
        return lax.dot_general(weighted, rows, NT, preferred_element_type=jnp.float32)

    def take_batch(i):
        s = lax.rem(me + n_shell - far_first(n_shell - 2 - i), n_shell)
        ang_copy(me, s).wait_recv()
        meta_copy(me, s).wait_recv()
        return add_batch(s)

    mom = accumulate(n_shell - 1, take_batch, add_batch(me))

    mom_h, mom_l = split2(mom)
    both = jnp.concatenate([mom_h.astype(jnp.float32), mom_l.astype(jnp.float32)], axis=0)
    row_ids = lax.broadcasted_iota(jnp.int32, (2 * lmp, width), 0)
    row_ids = jnp.where(row_ids >= lmp, row_ids - lmp, row_ids)
    spread = jnp.concatenate(
        [jnp.where((row_ids >= l * l) & (row_ids < (l + 1) * (l + 1)), both, 0.0)
         for l in range(degrees)], axis=1).astype(jnp.bfloat16)
    first = jnp.dot(spread, gh_v[...], preferred_element_type=jnp.float32)
    second = jnp.dot(spread[0:lmp], gl_v[...], preferred_element_type=jnp.float32)
    table = (first[0:lmp] + first[lmp:] + second).astype(jnp.bfloat16)

    def evaluate(b, out, at):
        radial = jnp.dot(table, rows_v[b], preferred_element_type=jnp.float32)
        out[at] = jnp.sum(rang[b].astype(jnp.float32) * radial, axis=0, keepdims=True)

    def evaluate_to(i):
        to = shell_at(far_first(i))
        evaluate(to, val_v, to)

    first_part = n_shell // 2
    for low, high in ((0, first_part), (first_part, n_shell - 1)):
        repeat(high - low, lambda i: evaluate_to(i + low))
        repeat(high - low, lambda i: val_copy(shell_at(far_first(i + low)), me).start())
    evaluate(me, rval, me)

    def placed(a):
        spot = jnp.where(coarse_ids == high_v[pl.ds(a, 1), :], rval[a], 0.0)
        spot_h, spot_l = split2(spot)
        spots = jnp.concatenate(
            [spot_h.astype(jnp.float32), spot_l.astype(jnp.float32)], axis=0).astype(jnp.bfloat16)
        return lax.dot_general(spots, onehot[a], NT, preferred_element_type=jnp.float32)

    repeat(n_shell - 1, lambda i: val_copy(me, shell_at(i + 1)).wait_recv())
    terms = accumulate(n_shell - 1, lambda i: placed(i + 1), placed(0))
    terms = terms[0:coarse] + terms[coarse:]
    share = coarse // n_atom
    for g in range(n_atom):
        part_v[g] = terms[g * share:(g + 1) * share]

    repeat(n_atom - 1, lambda i: part_copy(atom_at(i + 1), ma).start())
    rpart[ma] = part_v[ma]

    def take_part(i):
        part_copy(ma, atom_at(i + 1)).wait_recv()

    repeat(n_atom - 1, take_part)
    total = rpart[0]
    for g in range(1, n_atom):
        total = total + rpart[g]
    out_ref[...] = total

    def finish(i):
        to = shell_at(i + 1)
        ang_copy(to, me).wait_send()
        meta_copy(to, me).wait_send()
        val_copy(to, me).wait_send()

    repeat(n_shell - 1, finish)
    repeat(n_atom - 1, lambda i: part_copy(atom_at(i + 1), ma).wait_send())


def solution(mesh):
    n_shell, n_atom = mesh.shape["shell"], mesh.shape["atom"]

    def per_device(rho, task_point, task_count, radial_index, fraction, angular, green):
        _, atoms, lm, slots = angular.shape
        points = rho.shape[0]
        degrees, width, _ = green.shape
        assert atoms == n_shell and points % (LANES * n_atom) == 0
        assert degrees == math.isqrt(lm)
        coarse = points // LANES
        share = coarse // n_atom
        lmp = (lm // 16 + 1) * 16
        meta_rows = 3 + lm % 16
        f32, bf16, i32 = jnp.float32, jnp.bfloat16, jnp.int32
        vmem = pltpu.VMEM
        scratch = [
            vmem((coarse, LANES), f32),
            vmem((atoms, slots), i32),
            vmem((1, atoms), i32),
            vmem((atoms, slots), i32),
            vmem((atoms, slots), f32),
            vmem((lm, atoms, slots), bf16),
            vmem((slots // LANES, lm * atoms, LANES), f32),
            vmem((atoms, lm // 16 * 16, slots), bf16),
            vmem((degrees, width, width), f32),
            vmem((atoms, slots), f32),
            vmem((atoms, slots), i32),
            vmem((atoms, slots), i32),
            vmem((atoms, LANES, slots), bf16),
            vmem((atoms, meta_rows, slots), f32),
            vmem((n_shell, meta_rows, slots), f32),
            vmem((n_shell, lmp, slots), bf16),
            vmem((n_shell, width, slots), bf16),
            vmem((degrees * width, width), bf16),
            vmem((degrees * width, width), bf16),
            vmem((n_shell, 1, slots), f32),
            vmem((n_shell, 1, slots), f32),
            vmem((n_atom, share, LANES), f32),
            vmem((n_atom, share, LANES), f32),
            pltpu.SemaphoreType.DMA((7,)),
        ] + [pltpu.SemaphoreType.DMA((n_shell,))] * 6 + [pltpu.SemaphoreType.DMA((n_atom,))] * 2
        out = pl.pallas_call(
            functools.partial(kernel, n_shell, n_atom),
            out_shape=jax.ShapeDtypeStruct((share, LANES), f32),
            in_specs=[pl.BlockSpec(memory_space=pltpu.HBM)] * 7,
            out_specs=pl.BlockSpec(memory_space=pltpu.VMEM),
            scratch_shapes=scratch,
            compiler_params=pltpu.CompilerParams(
                collective_id=0, has_side_effects=True, vmem_limit_bytes=64 * 1024 * 1024),
            name="hartree",
        )(rho.reshape(coarse, LANES), task_point, task_count, radial_index, fraction,
          jnp.transpose(angular, (0, 2, 1, 3)), green)
        return out.reshape(share * LANES)

    in_specs = (
        P("shell"),
        P("shell", "atom", None),
        P("shell", "atom"),
        P("shell", "atom", None),
        P("shell", "atom", None),
        P("shell", "atom", None, None),
        P(),
    )
    return jax.shard_map(
        per_device, mesh=mesh, in_specs=in_specs, out_specs=P(("shell", "atom")), check_vma=False
    )
```

```python
import functools
import math

import jax
import jax.numpy as jnp
from jax import lax
from jax.experimental import pallas as pl
from jax.experimental.pallas import tpu as pltpu
from jax.sharding import PartitionSpec as P

MESH = pl.DeviceIdType.MESH
LANES = 128
NT = (((1,), (1,)), ((), ()))


def repeat(count, body):
    if count <= 16:
        for i in range(count):
            body(i)
    else:
        lax.fori_loop(0, count, lambda i, c: (body(i), c)[1], 0)


def accumulate(count, body, total):
    if count <= 16:
        for i in range(count):
            total = total + body(i)
        return total
    return lax.fori_loop(0, count, lambda i, c: c + body(i), total)


def split2(x):
    high = x.astype(jnp.bfloat16)
    low = (x - high.astype(jnp.float32)).astype(jnp.bfloat16)
    return high, low


def kernel(n_shell, n_atom, rho_h, pts_h, cnt_h, idx_h, frac_h, ang_h, green_h, out_ref,
           rho_v, pts_v, cnt_v, idx_v, frac_v, ang_s, ang_f, ang_v, green_v,
           live_v, low_v, high_v, onehot, meta_v, rmeta, rang, rows_v, gh_v, gl_v,
           mom_v, rmom, val_v, rval, part_v, rpart,
           local_sem, s_ang, r_ang, s_meta, r_meta, s_mom, r_mom, s_val, r_val, s_part, r_part):
    shell, ma = lax.axis_index("shell"), lax.axis_index("atom")
    half, own = val_v.shape[0], val_v.shape[1]
    me = lax.rem(shell, half)
    base = shell - me
    mirror = lax.rem(shell + half, n_shell)
    lm, atoms, slots = ang_s.shape
    lmp = rang.shape[2]
    body_rows = ang_v.shape[1]
    rest = lm - body_rows
    halves = slots // LANES
    degrees, width = green_v.shape[0], green_v.shape[1]
    coarse = rho_v.shape[0]

    def load(i, src, dst):
        copy = pltpu.make_async_copy(src, dst, local_sem.at[i])
        copy.start()
        return copy

    c_ang = load(0, ang_h.at[0], ang_s)
    c_pts = load(1, pts_h.at[0], pts_v)
    c_rho = load(2, rho_h, rho_v)
    c_idx = load(3, idx_h.at[0], idx_v)
    c_cnt = load(4, cnt_h, cnt_v)
    c_frac = load(5, frac_h.at[0], frac_v)
    c_green = load(6, green_h, green_v)

    def peer(k):
        return lax.rem(me + k, half)

    def atom_at(k):
        return lax.rem(ma + k, n_atom)

    def far_first(i):
        step = (i + 1) // 2
        return peer(half // 2 + step * (1 - 2 * (i % 2)))

    barrier = pltpu.get_barrier_semaphore()
    repeat(half - 1, lambda i: pl.semaphore_signal(
        barrier, inc=1, device_id=(base + peer(i + 1), ma), device_id_type=MESH))
    pl.semaphore_signal(barrier, inc=1, device_id=(mirror, ma), device_id_type=MESH)
    repeat(n_atom - 1, lambda i: pl.semaphore_signal(
        barrier, inc=1, device_id=(shell, atom_at(i + 1)), device_id_type=MESH))

    def ang_copy(t, to, slot):
        return pltpu.make_async_remote_copy(
            src_ref=ang_v.at[to * own + t], dst_ref=rang.at[t, slot, pl.ds(0, body_rows)],
            send_sem=s_ang.at[t, to], recv_sem=r_ang.at[t, slot],
            device_id=(base + to, ma), device_id_type=MESH)

    def meta_copy(to, slot):
        return pltpu.make_async_remote_copy(
            src_ref=meta_v.at[to], dst_ref=rmeta.at[slot],
            send_sem=s_meta.at[to], recv_sem=r_meta.at[slot],
            device_id=(base + to, ma), device_id_type=MESH)

    def mom_copy(t):
        return pltpu.make_async_remote_copy(
            src_ref=mom_v.at[t], dst_ref=rmom.at[t],
            send_sem=s_mom.at[t], recv_sem=r_mom.at[t],
            device_id=(mirror, ma), device_id_type=MESH)

    def val_copy(to, slot):
        return pltpu.make_async_remote_copy(
            src_ref=val_v.at[to], dst_ref=rval.at[slot],
            send_sem=s_val.at[to], recv_sem=r_val.at[slot],
            device_id=(base + to, ma), device_id_type=MESH)

    def part_copy(to, slot):
        return pltpu.make_async_remote_copy(
            src_ref=part_v.at[to], dst_ref=rpart.at[slot],
            send_sem=s_part.at[to], recv_sem=r_part.at[slot],
            device_id=(shell, to), device_id_type=MESH)

    c_ang.wait()

    def widen(m):
        at = pl.multiple_of(m * atoms, 8) if atoms % 8 == 0 else m * atoms
        for h in range(halves):
            ang_f[h, pl.ds(at, atoms), :] = ang_s[m, :, h * LANES:(h + 1) * LANES].astype(jnp.float32)

    def by_atom(a):
        for h in range(halves):
            ang_v[a, :, h * LANES:(h + 1) * LANES] = ang_f[
                h, pl.ds(a, body_rows, stride=atoms), :].astype(jnp.bfloat16)

    if atoms <= 16:
        for m in range(lm):
            widen(m)
    else:
        repeat(lm, widen)
    repeat(atoms, by_atom)
    pl.semaphore_wait(barrier, half + n_atom - 1)
    repeat(half - 1, lambda i: ang_copy(0, far_first(i), me).start())

    c_pts.wait()
    c_rho.wait()
    c_idx.wait()
    c_cnt.wait()
    c_frac.wait()
    low_v[...] = pts_v[...] & (LANES - 1)
    high_v[...] = pts_v[...] >> (LANES.bit_length() - 1)
    count_row = jnp.broadcast_to(cnt_v[...].astype(jnp.float32), (atoms, atoms))
    diagonal = (lax.broadcasted_iota(jnp.int32, (atoms, atoms), 0)
                == lax.broadcasted_iota(jnp.int32, (atoms, atoms), 1))
    counts = jnp.sum(jnp.where(diagonal, count_row, 0.0), axis=1, keepdims=True)
    slot_ids = lax.broadcasted_iota(jnp.int32, (atoms, slots), 1).astype(jnp.float32)
    live_v[...] = jnp.where(slot_ids < counts, idx_v[...].astype(jnp.float32), -8.0)

    rho = rho_v[...]
    rho_1 = rho.astype(jnp.bfloat16)
    rho_2, rho_3 = split2(rho - rho_1.astype(jnp.float32))
    rho_parts = jnp.concatenate(
        [rho_1.astype(jnp.float32), rho_2.astype(jnp.float32), rho_3.astype(jnp.float32)],
        axis=0).astype(jnp.bfloat16)
    fine_ids = lax.broadcasted_iota(jnp.int32, (LANES, slots), 0)
    coarse_ids = lax.broadcasted_iota(jnp.int32, (coarse, slots), 0)

    def build_meta(a):
        hot = jnp.where(fine_ids == low_v[pl.ds(a, 1), :], 1.0, 0.0).astype(jnp.bfloat16)
        onehot[a] = hot
        found = jnp.dot(rho_parts, hot, preferred_element_type=jnp.float32)
        found = found[0:coarse] + found[coarse:2 * coarse] + found[2 * coarse:3 * coarse]
        here = coarse_ids == high_v[pl.ds(a, 1), :]
        to, t = a // own, a % own
        meta_v[to, t, 0:1, :] = jnp.sum(jnp.where(here, found, 0.0), axis=0, keepdims=True)
        meta_v[to, t, 1:2, :] = live_v[pl.ds(a, 1), :]
        meta_v[to, t, 2:3, :] = frac_v[pl.ds(a, 1), :]
        for j in range(rest):
            for h in range(halves):
                meta_v[to, t, 3 + j:4 + j, h * LANES:(h + 1) * LANES] = ang_f[
                    h, pl.ds((body_rows + j) * atoms + a, 1), :]

    repeat(atoms, build_meta)
    repeat(half - 1, lambda i: meta_copy(far_first(i), me).start())
    for t in range(1, own):
        repeat(half - 1, lambda i: ang_copy(t, far_first(i), me).start())
    rmeta[me] = meta_v[me]
    for t in range(own):
        rang[t, me, 0:body_rows] = ang_v[me * own + t]

    c_green.wait()
    green = green_v[...].reshape(degrees * width, width)
    gh, gl = split2(green)
    gh_v[...] = gh
    gl_v[...] = gl

    grid_ids = lax.broadcasted_iota(jnp.int32, (width, slots), 0).astype(jnp.float32)
    tail_ids = lax.broadcasted_iota(jnp.int32, (lmp - body_rows, slots), 0)

    def add_batch(t, s):
        index, fraction = rmeta[s, t, 1:2, :], rmeta[s, t, 2:3, :]
        offset = grid_ids - index
        rows = jnp.where(offset == 0.0, 1.0 - fraction, jnp.where(offset == 1.0, fraction, 0.0))
        rows = rows.astype(jnp.bfloat16)
        rows_v[t, s] = rows
        tail = jnp.zeros((lmp - body_rows, slots), jnp.float32)
        for j in range(rest):
            tail = jnp.where(tail_ids == j, rmeta[s, t, 3 + j:4 + j, :], tail)
        rang[t, s, body_rows:lmp] = tail.astype(jnp.bfloat16)
        weighted = (rang[t, s].astype(jnp.float32) * rmeta[s, t, 0:1, :]).astype(jnp.bfloat16)
        return lax.dot_general(weighted, rows, NT, preferred_element_type=jnp.float32)

    def take_batch(t, i):
        s = peer(i + 1)
        if t == 0:
            meta_copy(me, s).wait_recv()
        ang_copy(t, me, s).wait_recv()
        return add_batch(t, s)

    partial = [add_batch(t, me) for t in range(own)]
    for t in range(own):
        partial[t] = accumulate(half - 1, functools.partial(take_batch, t), partial[t])
        mom_v[t] = partial[t].astype(jnp.bfloat16)
        mom_copy(t).start()

    row_ids = lax.broadcasted_iota(jnp.int32, (2 * lmp, width), 0)
    row_ids = jnp.where(row_ids >= lmp, row_ids - lmp, row_ids)

    def solve(mom):
        mom_h, mom_l = split2(mom)
        both = jnp.concatenate([mom_h.astype(jnp.float32), mom_l.astype(jnp.float32)], axis=0)
        spread = jnp.concatenate(
            [jnp.where((row_ids >= l * l) & (row_ids < (l + 1) * (l + 1)), both, 0.0)
             for l in range(degrees)], axis=1).astype(jnp.bfloat16)
        first = jnp.dot(spread, gh_v[...], preferred_element_type=jnp.float32)
        second = jnp.dot(spread[0:lmp], gl_v[...], preferred_element_type=jnp.float32)
        return (first[0:lmp] + first[lmp:] + second).astype(jnp.bfloat16)

    for t in range(own):
        mom_copy(t).wait_recv()
        table = solve(partial[t] + rmom[t].astype(jnp.float32))

        def evaluate(b, out):
            radial = jnp.dot(table, rows_v[t, b], preferred_element_type=jnp.float32)
            out[b, t] = jnp.sum(rang[t, b].astype(jnp.float32) * radial, axis=0, keepdims=True)

        repeat(half - 1, lambda i: evaluate(far_first(i), val_v))
        if t == own - 1:
            repeat(half - 1, lambda i: val_copy(far_first(i), me).start())
        evaluate(me, rval)

    def placed(a):
        spot = jnp.where(coarse_ids == high_v[pl.ds(a, 1), :], rval[a // own, a % own], 0.0)
        spot_h, spot_l = split2(spot)
        spots = jnp.concatenate(
            [spot_h.astype(jnp.float32), spot_l.astype(jnp.float32)], axis=0).astype(jnp.bfloat16)
        return lax.dot_general(spots, onehot[a], NT, preferred_element_type=jnp.float32)

    repeat(half - 1, lambda i: val_copy(me, peer(i + 1)).wait_recv())
    terms = accumulate(atoms - 1, lambda i: placed(i + 1), placed(0))
    terms = terms[0:coarse] + terms[coarse:]
    share = coarse // n_atom
    for g in range(n_atom):
        part_v[g] = terms[g * share:(g + 1) * share]

    repeat(n_atom - 1, lambda i: part_copy(atom_at(i + 1), ma).start())
    rpart[ma] = part_v[ma]
    repeat(n_atom - 1, lambda i: part_copy(ma, atom_at(i + 1)).wait_recv())
    total = rpart[0]
    for g in range(1, n_atom):
        total = total + rpart[g]
    out_ref[...] = total

    def finish(i):
        to = peer(i + 1)
        for t in range(own):
            ang_copy(t, to, me).wait_send()
        meta_copy(to, me).wait_send()
        val_copy(to, me).wait_send()

    repeat(half - 1, finish)
    for t in range(own):
        mom_copy(t).wait_send()
    repeat(n_atom - 1, lambda i: part_copy(atom_at(i + 1), ma).wait_send())


def solution(mesh):
    n_shell, n_atom = mesh.shape["shell"], mesh.shape["atom"]

    def per_device(rho, task_point, task_count, radial_index, fraction, angular, green):
        _, atoms, lm, slots = angular.shape
        points = rho.shape[0]
        degrees, width, _ = green.shape
        half = n_shell // 2
        own = atoms // half
        assert n_shell % 2 == 0 and atoms == half * own and points % (LANES * n_atom) == 0
        assert degrees == math.isqrt(lm)
        coarse = points // LANES
        share = coarse // n_atom
        lmp = (lm // 16 + 1) * 16
        meta_rows = 3 + lm % 16
        f32, bf16, i32 = jnp.float32, jnp.bfloat16, jnp.int32
        vmem = pltpu.VMEM
        scratch = [
            vmem((coarse, LANES), f32),
            vmem((atoms, slots), i32),
            vmem((1, atoms), i32),
            vmem((atoms, slots), i32),
            vmem((atoms, slots), f32),
            vmem((lm, atoms, slots), bf16),
            vmem((slots // LANES, lm * atoms, LANES), f32),
            vmem((atoms, lm // 16 * 16, slots), bf16),
            vmem((degrees, width, width), f32),
            vmem((atoms, slots), f32),
            vmem((atoms, slots), i32),
            vmem((atoms, slots), i32),
            vmem((atoms, LANES, slots), bf16),
            vmem((half, own, meta_rows, slots), f32),
            vmem((half, own, meta_rows, slots), f32),
            vmem((own, half, lmp, slots), bf16),
            vmem((own, half, width, slots), bf16),
            vmem((degrees * width, width), bf16),
            vmem((degrees * width, width), bf16),
            vmem((own, lmp, width), bf16),
            vmem((own, lmp, width), bf16),
            vmem((half, own, 1, slots), f32),
            vmem((half, own, 1, slots), f32),
            vmem((n_atom, share, LANES), f32),
            vmem((n_atom, share, LANES), f32),
        ] + [pltpu.SemaphoreType.DMA(shape) for shape in (
            (7,), (own, half), (own, half), (half,), (half,), (own,), (own,), (half,), (half,),
            (n_atom,), (n_atom,))]
        out = pl.pallas_call(
            functools.partial(kernel, n_shell, n_atom),
            out_shape=jax.ShapeDtypeStruct((share, LANES), f32),
            in_specs=[pl.BlockSpec(memory_space=pltpu.HBM)] * 7,
            out_specs=pl.BlockSpec(memory_space=pltpu.VMEM),
            scratch_shapes=scratch,
            compiler_params=pltpu.CompilerParams(
                collective_id=0, has_side_effects=True, vmem_limit_bytes=64 * 1024 * 1024),
            name="hartree",
        )(rho.reshape(coarse, LANES), task_point, task_count, radial_index, fraction,
          jnp.transpose(angular, (0, 2, 1, 3)), green)
        return out.reshape(share * LANES)

    in_specs = (
        P("shell"),
        P("shell", "atom", None),
        P("shell", "atom"),
        P("shell", "atom", None),
        P("shell", "atom", None),
        P("shell", "atom", None, None),
        P(),
    )
    return jax.shard_map(
        per_device, mesh=mesh, in_specs=in_specs, out_specs=P(("shell", "atom")), check_vma=False
    )
```

```python
import functools
import math

import jax
import jax.numpy as jnp
from jax import lax
from jax.experimental import pallas as pl
from jax.experimental.pallas import tpu as pltpu
from jax.sharding import PartitionSpec as P

MESH = pl.DeviceIdType.MESH
LANES = 128
FINE = 32
NT = (((1,), (1,)), ((), ()))


def repeat(count, body):
    if count <= 16:
        for i in range(count):
            body(i)
    else:
        lax.fori_loop(0, count, lambda i, c: (body(i), c)[1], 0)


def accumulate(count, body, total):
    if count <= 16:
        for i in range(count):
            total = total + body(i)
        return total
    return lax.fori_loop(0, count, lambda i, c: c + body(i), total)


def split2(x):
    high = x.astype(jnp.bfloat16)
    low = (x - high.astype(jnp.float32)).astype(jnp.bfloat16)
    return high, low


def kernel(n_shell, n_atom, rho_h, pts_h, cnt_h, idx_h, frac_h, ang_h, green_h, out_ref,
           rho_v, pts_v, cnt_v, idx_v, frac_v, ang_s, ang_f, ang_v, green_v,
           live_v, low_v, high_v, rpts, spot_v, onehot, meta_v, rmeta, rang, rows_v, gh_v, gl_v,
           mom_v, rmom, val_v, rval,
           local_sem, s_ang, r_ang, s_meta, r_meta, s_mom, r_mom, s_val, r_val, s_pts, r_pts):
    shell, ma = lax.axis_index("shell"), lax.axis_index("atom")
    half, own = val_v.shape[0], val_v.shape[1]
    me = lax.rem(shell, half)
    base = shell - me
    mirror = lax.rem(shell + half, n_shell)
    lm, atoms, slots = ang_s.shape
    lmp = rang.shape[2]
    body_rows = ang_v.shape[1]
    rest = lm - body_rows
    halves = slots // LANES
    degrees, width = green_v.shape[0], green_v.shape[1]
    coarse = rho_v.shape[0]

    def load(i, src, dst):
        copy = pltpu.make_async_copy(src, dst, local_sem.at[i])
        copy.start()
        return copy

    c_ang = load(0, ang_h.at[0], ang_s)
    c_pts = load(1, pts_h.at[0], pts_v)
    c_rho = load(2, rho_h, rho_v)
    c_idx = load(3, idx_h.at[0], idx_v)
    c_cnt = load(4, cnt_h, cnt_v)
    c_frac = load(5, frac_h.at[0], frac_v)
    c_green = load(6, green_h, green_v)

    def peer(k):
        return lax.rem(me + k, half)

    def atom_at(k):
        return lax.rem(ma + k, n_atom)

    def far_first(i):
        step = (i + 1) // 2
        return peer(half // 2 + step * (1 - 2 * (i % 2)))

    barrier = pltpu.get_barrier_semaphore()
    repeat(half - 1, lambda i: pl.semaphore_signal(
        barrier, inc=1, device_id=(base + peer(i + 1), ma), device_id_type=MESH))
    pl.semaphore_signal(barrier, inc=1, device_id=(mirror, ma), device_id_type=MESH)
    for k in range(1, n_atom):
        repeat(half, lambda i: pl.semaphore_signal(
            barrier, inc=1, device_id=(base + peer(i), atom_at(k)), device_id_type=MESH))

    def ang_copy(t, to, slot):
        return pltpu.make_async_remote_copy(
            src_ref=ang_v.at[to * own + t], dst_ref=rang.at[t, slot, pl.ds(0, body_rows)],
            send_sem=s_ang.at[t, to], recv_sem=r_ang.at[t, slot],
            device_id=(base + to, ma), device_id_type=MESH)

    def meta_copy(to, slot):
        return pltpu.make_async_remote_copy(
            src_ref=meta_v.at[to], dst_ref=rmeta.at[slot],
            send_sem=s_meta.at[to], recv_sem=r_meta.at[slot],
            device_id=(base + to, ma), device_id_type=MESH)

    def mom_copy(t):
        return pltpu.make_async_remote_copy(
            src_ref=mom_v.at[t], dst_ref=rmom.at[t],
            send_sem=s_mom.at[t], recv_sem=r_mom.at[t],
            device_id=(mirror, ma), device_id_type=MESH)

    def val_copy(to, group, slot, from_group):
        return pltpu.make_async_remote_copy(
            src_ref=val_v.at[to], dst_ref=rval.at[from_group, slot],
            send_sem=s_val.at[group, to], recv_sem=r_val.at[from_group, slot],
            device_id=(base + to, group), device_id_type=MESH)

    def pts_copy(group, slot):
        return pltpu.make_async_remote_copy(
            src_ref=pts_v, dst_ref=rpts.at[slot],
            send_sem=s_pts.at[group], recv_sem=r_pts.at[slot],
            device_id=(shell, group), device_id_type=MESH)

    c_ang.wait()

    def widen(m):
        at = pl.multiple_of(m * atoms, 8) if atoms % 8 == 0 else m * atoms
        for h in range(halves):
            ang_f[h, pl.ds(at, atoms), :] = ang_s[m, :, h * LANES:(h + 1) * LANES].astype(jnp.float32)

    def by_atom(a):
        for h in range(halves):
            ang_v[a, :, h * LANES:(h + 1) * LANES] = ang_f[
                h, pl.ds(a, body_rows, stride=atoms), :].astype(jnp.bfloat16)

    if atoms <= 16:
        for m in range(lm):
            widen(m)
    else:
        repeat(lm, widen)
    repeat(atoms, by_atom)
    pl.semaphore_wait(barrier, half * n_atom)
    repeat(half - 1, lambda i: ang_copy(0, far_first(i), me).start())

    c_pts.wait()
    repeat(n_atom - 1, lambda i: pts_copy(atom_at(i + 1), ma).start())
    c_rho.wait()
    c_idx.wait()
    c_cnt.wait()
    c_frac.wait()
    low_v[...] = pts_v[...] & (LANES - 1)
    high_v[...] = pts_v[...] >> (LANES.bit_length() - 1)
    count_row = jnp.broadcast_to(cnt_v[...].astype(jnp.float32), (atoms, atoms))
    diagonal = (lax.broadcasted_iota(jnp.int32, (atoms, atoms), 0)
                == lax.broadcasted_iota(jnp.int32, (atoms, atoms), 1))
    counts = jnp.sum(jnp.where(diagonal, count_row, 0.0), axis=1, keepdims=True)
    slot_ids = lax.broadcasted_iota(jnp.int32, (atoms, slots), 1).astype(jnp.float32)
    live_v[...] = jnp.where(slot_ids < counts, idx_v[...].astype(jnp.float32), -8.0)

    rho = rho_v[...]
    rho_1 = rho.astype(jnp.bfloat16)
    rho_2, rho_3 = split2(rho - rho_1.astype(jnp.float32))
    rho_parts = jnp.concatenate(
        [rho_1.astype(jnp.float32), rho_2.astype(jnp.float32), rho_3.astype(jnp.float32)],
        axis=0).astype(jnp.bfloat16)
    fine_ids = lax.broadcasted_iota(jnp.int32, (LANES, slots), 0)
    coarse_ids = lax.broadcasted_iota(jnp.int32, (coarse, slots), 0)

    def build_meta(a):
        hot = jnp.where(fine_ids == low_v[pl.ds(a, 1), :], 1.0, 0.0).astype(jnp.bfloat16)
        found = jnp.dot(rho_parts, hot, preferred_element_type=jnp.float32)
        found = found[0:coarse] + found[coarse:2 * coarse] + found[2 * coarse:3 * coarse]
        here = coarse_ids == high_v[pl.ds(a, 1), :]
        to, t = a // own, a % own
        meta_v[to, t, 0:1, :] = jnp.sum(jnp.where(here, found, 0.0), axis=0, keepdims=True)
        meta_v[to, t, 1:2, :] = live_v[pl.ds(a, 1), :]
        meta_v[to, t, 2:3, :] = frac_v[pl.ds(a, 1), :]
        for j in range(rest):
            for h in range(halves):
                meta_v[to, t, 3 + j:4 + j, h * LANES:(h + 1) * LANES] = ang_f[
                    h, pl.ds((body_rows + j) * atoms + a, 1), :]

    repeat(atoms, build_meta)
    repeat(half - 1, lambda i: meta_copy(far_first(i), me).start())
    for t in range(1, own):
        repeat(half - 1, lambda i: ang_copy(t, far_first(i), me).start())
    rmeta[me] = meta_v[me]
    rpts[ma] = pts_v[...]
    for t in range(own):
        rang[t, me, 0:body_rows] = ang_v[me * own + t]

    c_green.wait()
    green = green_v[...].reshape(degrees * width, width)
    gh, gl = split2(green)
    gh_v[...] = gh
    gl_v[...] = gl

    grid_ids = lax.broadcasted_iota(jnp.int32, (width, slots), 0).astype(jnp.float32)
    tail_ids = lax.broadcasted_iota(jnp.int32, (lmp - body_rows, slots), 0)

    def add_batch(t, s):
        index, fraction = rmeta[s, t, 1:2, :], rmeta[s, t, 2:3, :]
        offset = grid_ids - index
        rows = jnp.where(offset == 0.0, 1.0 - fraction, jnp.where(offset == 1.0, fraction, 0.0))
        rows = rows.astype(jnp.bfloat16)
        rows_v[t, s] = rows
        tail = jnp.zeros((lmp - body_rows, slots), jnp.float32)
        for j in range(rest):
            tail = jnp.where(tail_ids == j, rmeta[s, t, 3 + j:4 + j, :], tail)
        rang[t, s, body_rows:lmp] = tail.astype(jnp.bfloat16)
        weighted = (rang[t, s].astype(jnp.float32) * rmeta[s, t, 0:1, :]).astype(jnp.bfloat16)
        return lax.dot_general(weighted, rows, NT, preferred_element_type=jnp.float32)

    def take_batch(t, i):
        s = peer(i + 1)
        if t == 0:
            meta_copy(me, s).wait_recv()
        ang_copy(t, me, s).wait_recv()
        return add_batch(t, s)

    partial = [add_batch(t, me) for t in range(own)]
    for t in range(own):
        partial[t] = accumulate(half - 1, functools.partial(take_batch, t), partial[t])
        mom_v[t] = partial[t].astype(jnp.bfloat16)
        mom_copy(t).start()

    share = out_ref.shape[0]
    cells = LANES // FINE
    cell_ids = lax.broadcasted_iota(jnp.int32, (FINE, slots), 0)

    def find_spots(k):
        group = atom_at(k)
        if k > 0:
            pts_copy(ma, group).wait_recv()
        at = rpts[group] - ma * (share * LANES)
        block = at >> (LANES.bit_length() - 1)
        inside = (block >= 0) & (block < share)
        cell = (at >> (FINE.bit_length() - 1)) & (cells - 1)
        spot_v[group] = jnp.where(inside, cell * share + block, -1)
        rpts[group] = at & (FINE - 1)

        def mark(a):
            column = rpts[group, pl.ds(a, 1), :]
            onehot[group, a] = jnp.where(cell_ids == column, 1.0, 0.0).astype(jnp.bfloat16)

        repeat(atoms, mark)

    for k in range(n_atom):
        find_spots(k)

    def spread_of(mom):
        rows = mom.shape[0]
        ids = lax.broadcasted_iota(jnp.int32, (rows, width), 0)
        ids = jnp.where(ids >= lmp, ids - lmp, ids)
        return jnp.concatenate(
            [jnp.where((ids >= l * l) & (ids < (l + 1) * (l + 1)), mom, 0.0)
             for l in range(degrees)], axis=1).astype(jnp.bfloat16)

    solved = []
    for t in range(own):
        mom_h, mom_l = split2(partial[t])
        spread = spread_of(
            jnp.concatenate([mom_h.astype(jnp.float32), mom_l.astype(jnp.float32)], axis=0))
        first = jnp.dot(spread, gh_v[...], preferred_element_type=jnp.float32)
        second = jnp.dot(spread[0:lmp], gl_v[...], preferred_element_type=jnp.float32)
        solved.append(first[0:lmp] + first[lmp:] + second)

    for t in range(own):
        mom_copy(t).wait_recv()
        spread = spread_of(rmom[t].astype(jnp.float32))
        other = (jnp.dot(spread, gh_v[...], preferred_element_type=jnp.float32)
                 + jnp.dot(spread, gl_v[...], preferred_element_type=jnp.float32))
        table = (solved[t] + other).astype(jnp.bfloat16)

        def evaluate(b):
            radial = jnp.dot(table, rows_v[t, b], preferred_element_type=jnp.float32)
            val_v[b, t] = jnp.sum(rang[t, b].astype(jnp.float32) * radial, axis=0, keepdims=True)

        repeat(half - 1, lambda i: evaluate(far_first(i)))
        evaluate(me)
    repeat(half - 1, lambda i: val_copy(far_first(i), ma, me, ma).start())
    for k in range(1, n_atom):
        repeat(half, lambda i: val_copy(peer(half - 1 - i), atom_at(k), me, ma).start())
    rval[ma, me] = val_v[me]

    spot_ids = lax.broadcasted_iota(jnp.int32, (cells * share, slots), 0)

    def add_group(k, terms):
        group = atom_at(k)
        if k == 0:
            repeat(half - 1, lambda i: val_copy(me, ma, peer(i + 1), ma).wait_recv())
        else:
            repeat(half, lambda i: val_copy(me, ma, peer(i), group).wait_recv())

        def placed(a):
            here = spot_ids == spot_v[group, pl.ds(a, 1), :]
            spot = jnp.where(here, rval[group, a // own, a % own], 0.0)
            spot_h, spot_l = split2(spot)
            spots = jnp.concatenate(
                [spot_h.astype(jnp.float32), spot_l.astype(jnp.float32)], axis=0).astype(jnp.bfloat16)
            return lax.dot_general(spots, onehot[group, a], NT, preferred_element_type=jnp.float32)

        return accumulate(atoms, placed, terms)

    terms = jnp.zeros((2 * cells * share, FINE), jnp.float32)
    for k in range(n_atom):
        terms = add_group(k, terms)
    terms = terms[0:cells * share] + terms[cells * share:]
    out_ref[...] = jnp.concatenate(
        [terms[c * share:(c + 1) * share] for c in range(cells)], axis=1)

    def finish(i):
        to = peer(i + 1)
        for t in range(own):
            ang_copy(t, to, me).wait_send()
        meta_copy(to, me).wait_send()
        val_copy(to, ma, me, ma).wait_send()

    repeat(half - 1, finish)
    for t in range(own):
        mom_copy(t).wait_send()
    for k in range(1, n_atom):
        pts_copy(atom_at(k), ma).wait_send()
        repeat(half, lambda i: val_copy(peer(i), atom_at(k), me, ma).wait_send())


def solution(mesh):
    n_shell, n_atom = mesh.shape["shell"], mesh.shape["atom"]

    def per_device(rho, task_point, task_count, radial_index, fraction, angular, green):
        _, atoms, lm, slots = angular.shape
        points = rho.shape[0]
        degrees, width, _ = green.shape
        half = n_shell // 2
        own = atoms // half
        assert n_shell % 2 == 0 and atoms == half * own and points % (LANES * n_atom) == 0
        assert degrees == math.isqrt(lm)
        coarse = points // LANES
        share = coarse // n_atom
        lmp = (lm // 16 + 1) * 16
        meta_rows = 3 + lm % 16
        f32, bf16, i32 = jnp.float32, jnp.bfloat16, jnp.int32
        vmem = pltpu.VMEM
        scratch = [
            vmem((coarse, LANES), f32),
            vmem((atoms, slots), i32),
            vmem((1, atoms), i32),
            vmem((atoms, slots), i32),
            vmem((atoms, slots), f32),
            vmem((lm, atoms, slots), bf16),
            vmem((slots // LANES, lm * atoms, LANES), f32),
            vmem((atoms, lm // 16 * 16, slots), bf16),
            vmem((degrees, width, width), f32),
            vmem((atoms, slots), f32),
            vmem((atoms, slots), i32),
            vmem((atoms, slots), i32),
            vmem((n_atom, atoms, slots), i32),
            vmem((n_atom, atoms, slots), i32),
            vmem((n_atom, atoms, FINE, slots), bf16),
            vmem((half, own, meta_rows, slots), f32),
            vmem((half, own, meta_rows, slots), f32),
            vmem((own, half, lmp, slots), bf16),
            vmem((own, half, width, slots), bf16),
            vmem((degrees * width, width), bf16),
            vmem((degrees * width, width), bf16),
            vmem((own, lmp, width), bf16),
            vmem((own, lmp, width), bf16),
            vmem((half, own, 1, slots), f32),
            vmem((n_atom, half, own, 1, slots), f32),
        ] + [pltpu.SemaphoreType.DMA(shape) for shape in (
            (7,), (own, half), (own, half), (half,), (half,), (own,), (own,), (n_atom, half),
            (n_atom, half), (n_atom,), (n_atom,))]
        out = pl.pallas_call(
            functools.partial(kernel, n_shell, n_atom),
            out_shape=pltpu.VMEM((share, LANES), f32),
            in_specs=[pl.BlockSpec(memory_space=pltpu.HBM)] * 7,
            out_specs=pl.BlockSpec(memory_space=pltpu.VMEM),
            scratch_shapes=scratch,
            compiler_params=pltpu.CompilerParams(
                collective_id=0, has_side_effects=True, vmem_limit_bytes=48 * 1024 * 1024),
            name="hartree",
        )(*[pltpu.with_memory_space_constraint(x, pltpu.HBM) for x in (
            rho.reshape(coarse, LANES), task_point, task_count, radial_index, fraction,
            jnp.transpose(angular, (0, 2, 1, 3)), green)])
        return out.reshape(share * LANES)

    in_specs = (
        P("shell"),
        P("shell", "atom", None),
        P("shell", "atom"),
        P("shell", "atom", None),
        P("shell", "atom", None),
        P("shell", "atom", None, None),
        P(),
    )
    return jax.shard_map(
        per_device, mesh=mesh, in_specs=in_specs, out_specs=P(("shell", "atom")), check_vma=False
    )
```

```python
import functools
import math

import jax
import jax.numpy as jnp
from jax import lax
from jax.experimental import pallas as pl
from jax.experimental.pallas import tpu as pltpu
from jax.sharding import PartitionSpec as P

MESH = pl.DeviceIdType.MESH
LANES = 128
FINE = 32
PIECES = 4
NT = (((1,), (1,)), ((), ()))


def repeat(count, body):
    if count <= 16:
        for i in range(count):
            body(i)
    else:
        lax.fori_loop(0, count, lambda i, c: (body(i), c)[1], 0)


def accumulate(count, body, total):
    if count <= 16:
        for i in range(count):
            total = total + body(i)
        return total
    return lax.fori_loop(0, count, lambda i, c: c + body(i), total)


def split2(x):
    high = x.astype(jnp.bfloat16)
    low = (x - high.astype(jnp.float32)).astype(jnp.bfloat16)
    return high, low


def kernel(n_shell, n_atom, rho_h, pts_h, cnt_h, idx_h, frac_h, ang_h, green_h, out_ref,
           rho_v, pts_v, cnt_v, idx_v, frac_v, ang_s, ang_f, ang_v, green_v,
           live_v, low_v, high_v, rpts, spot_v, onehot, meta_v, rmeta, rang, rows_v, green_2,
           mom_v, rmom, val_v, rval,
           local_sem, s_ang, r_ang, s_meta, r_meta, s_mom, r_mom, s_val, r_val, s_pts, r_pts):
    shell, ma = lax.axis_index("shell"), lax.axis_index("atom")
    half, own = val_v.shape[0], val_v.shape[1]
    me = lax.rem(shell, half)
    base = shell - me
    mirror = lax.rem(shell + half, n_shell)
    lm, atoms, slots = ang_s.shape
    lmp = rang.shape[2]
    body_rows = ang_v.shape[1]
    rest = lm - body_rows
    halves = slots // LANES
    degrees, width = green_v.shape[0], green_v.shape[1]
    coarse = rho_v.shape[0]

    def load(i, src, dst):
        copy = pltpu.make_async_copy(src, dst, local_sem.at[i])
        copy.start()
        return copy

    bounds = [lm * i // PIECES for i in range(PIECES + 1)]
    c_ang = [load(6 + i, ang_h.at[0, pl.ds(low, high - low)], ang_s.at[pl.ds(low, high - low)])
             for i, (low, high) in enumerate(zip(bounds, bounds[1:]))]
    c_pts = load(0, pts_h.at[0], pts_v)
    c_rho = load(1, rho_h, rho_v)
    c_idx = load(2, idx_h.at[0], idx_v)
    c_cnt = load(3, cnt_h, cnt_v)
    c_frac = load(4, frac_h.at[0], frac_v)

    def peer(k):
        return lax.rem(me + k, half)

    def atom_at(k):
        return lax.rem(ma + k, n_atom)

    def far_first(i):
        step = (i + 1) // 2
        return peer(half // 2 + step * (1 - 2 * (i % 2)))

    barrier = pltpu.get_barrier_semaphore()
    repeat(half - 1, lambda i: pl.semaphore_signal(
        barrier, inc=1, device_id=(base + peer(i + 1), ma), device_id_type=MESH))
    pl.semaphore_signal(barrier, inc=1, device_id=(mirror, ma), device_id_type=MESH)
    for k in range(1, n_atom):
        repeat(half, lambda i: pl.semaphore_signal(
            barrier, inc=1, device_id=(base + peer(i), atom_at(k)), device_id_type=MESH))
    c_green = load(5, green_h, green_v)

    def ang_copy(t, to, slot):
        return pltpu.make_async_remote_copy(
            src_ref=ang_v.at[to * own + t], dst_ref=rang.at[t, slot, pl.ds(0, body_rows)],
            send_sem=s_ang.at[t, to], recv_sem=r_ang.at[t, slot],
            device_id=(base + to, ma), device_id_type=MESH)

    def meta_copy(to, slot):
        return pltpu.make_async_remote_copy(
            src_ref=meta_v.at[to], dst_ref=rmeta.at[slot],
            send_sem=s_meta.at[to], recv_sem=r_meta.at[slot],
            device_id=(base + to, ma), device_id_type=MESH)

    def mom_copy(t):
        return pltpu.make_async_remote_copy(
            src_ref=mom_v.at[t], dst_ref=rmom.at[t],
            send_sem=s_mom.at[t], recv_sem=r_mom.at[t],
            device_id=(mirror, ma), device_id_type=MESH)

    def val_copy(to, group, slot, from_group):
        return pltpu.make_async_remote_copy(
            src_ref=val_v.at[to], dst_ref=rval.at[from_group, slot],
            send_sem=s_val.at[group, to], recv_sem=r_val.at[from_group, slot],
            device_id=(base + to, group), device_id_type=MESH)

    def pts_copy(group, slot):
        return pltpu.make_async_remote_copy(
            src_ref=pts_v, dst_ref=rpts.at[slot],
            send_sem=s_pts.at[group], recv_sem=r_pts.at[slot],
            device_id=(shell, group), device_id_type=MESH)

    def widen(m):
        at = pl.multiple_of(m * atoms, 8) if atoms % 8 == 0 else m * atoms
        for h in range(halves):
            ang_f[h, pl.ds(at, atoms), :] = ang_s[m, :, h * LANES:(h + 1) * LANES].astype(jnp.float32)

    def by_atom(a):
        for h in range(halves):
            ang_v[a, :, h * LANES:(h + 1) * LANES] = ang_f[
                h, pl.ds(a, body_rows, stride=atoms), :].astype(jnp.bfloat16)

    for copy, low, high in zip(c_ang, bounds, bounds[1:]):
        copy.wait()
        repeat(high - low, lambda i: widen(low + i))
    repeat(atoms, by_atom)
    pl.semaphore_wait(barrier, half * n_atom)
    repeat(half - 1, lambda i: ang_copy(0, far_first(i), me).start())

    c_pts.wait()
    repeat(n_atom - 1, lambda i: pts_copy(atom_at(i + 1), ma).start())
    c_rho.wait()
    c_idx.wait()
    c_cnt.wait()
    c_frac.wait()
    low_v[...] = pts_v[...] & (LANES - 1)
    high_v[...] = pts_v[...] >> (LANES.bit_length() - 1)
    count_row = jnp.broadcast_to(cnt_v[...].astype(jnp.float32), (atoms, atoms))
    diagonal = (lax.broadcasted_iota(jnp.int32, (atoms, atoms), 0)
                == lax.broadcasted_iota(jnp.int32, (atoms, atoms), 1))
    counts = jnp.sum(jnp.where(diagonal, count_row, 0.0), axis=1, keepdims=True)
    slot_ids = lax.broadcasted_iota(jnp.int32, (atoms, slots), 1).astype(jnp.float32)
    live_v[...] = jnp.where(slot_ids < counts, idx_v[...].astype(jnp.float32), -8.0)

    rho = rho_v[...]
    rho_1 = rho.astype(jnp.bfloat16)
    rho_2, rho_3 = split2(rho - rho_1.astype(jnp.float32))
    rho_parts = jnp.concatenate(
        [rho_1.astype(jnp.float32), rho_2.astype(jnp.float32), rho_3.astype(jnp.float32)],
        axis=0).astype(jnp.bfloat16)
    fine_ids = lax.broadcasted_iota(jnp.int32, (LANES, slots), 0)
    coarse_ids = lax.broadcasted_iota(jnp.int32, (coarse, slots), 0)

    def build_meta(a):
        hot = jnp.where(fine_ids == low_v[pl.ds(a, 1), :], 1.0, 0.0).astype(jnp.bfloat16)
        found = jnp.dot(rho_parts, hot, preferred_element_type=jnp.float32)
        found = found[0:coarse] + found[coarse:2 * coarse] + found[2 * coarse:3 * coarse]
        here = coarse_ids == high_v[pl.ds(a, 1), :]
        to, t = a // own, a % own
        meta_v[to, t, 0:1, :] = jnp.sum(jnp.where(here, found, 0.0), axis=0, keepdims=True)
        meta_v[to, t, 1:2, :] = live_v[pl.ds(a, 1), :]
        meta_v[to, t, 2:3, :] = frac_v[pl.ds(a, 1), :]
        for j in range(rest):
            for h in range(halves):
                meta_v[to, t, 3 + j:4 + j, h * LANES:(h + 1) * LANES] = ang_f[
                    h, pl.ds((body_rows + j) * atoms + a, 1), :]

    repeat(atoms, build_meta)
    repeat(half - 1, lambda i: meta_copy(far_first(i), me).start())
    for t in range(1, own):
        repeat(half - 1, lambda i: ang_copy(t, far_first(i), me).start())
    rmeta[me] = meta_v[me]
    rpts[ma] = pts_v[...]
    for t in range(own):
        rang[t, me, 0:body_rows] = ang_v[me * own + t]

    c_green.wait()
    green = green_v[...].reshape(degrees * width, width)
    gh, gl = split2(green)
    green_2[:, 0:width] = gh
    green_2[:, width:2 * width] = gl

    grid_ids = lax.broadcasted_iota(jnp.int32, (width, slots), 0).astype(jnp.float32)
    tail_ids = lax.broadcasted_iota(jnp.int32, (lmp - body_rows, slots), 0)

    def make_rows(t, s):
        index, fraction = rmeta[s, t, 1:2, :], rmeta[s, t, 2:3, :]
        offset = grid_ids - index
        rows = jnp.where(offset == 0.0, 1.0 - fraction, jnp.where(offset == 1.0, fraction, 0.0))
        rows_v[t, s] = rows.astype(jnp.bfloat16)
        tail = jnp.zeros((lmp - body_rows, slots), jnp.float32)
        for j in range(rest):
            tail = jnp.where(tail_ids == j, rmeta[s, t, 3 + j:4 + j, :], tail)
        rang[t, s, body_rows:lmp] = tail.astype(jnp.bfloat16)

    def add_batch(t, s):
        weighted = (rang[t, s].astype(jnp.float32) * rmeta[s, t, 0:1, :]).astype(jnp.bfloat16)
        return lax.dot_general(weighted, rows_v[t, s], NT, preferred_element_type=jnp.float32)

    def take_batch(t, i):
        s = peer(i + 1)
        if t == 0:
            meta_copy(me, s).wait_recv()
            make_rows(t, s)
        ang_copy(t, me, s).wait_recv()
        return add_batch(t, s)

    def solve(mom):
        rows = mom.shape[0]
        ids = lax.broadcasted_iota(jnp.int32, (rows, width), 0)
        ids = jnp.where(ids >= lmp, ids - lmp, ids)
        spread = jnp.concatenate(
            [jnp.where((ids >= l * l) & (ids < (l + 1) * (l + 1)), mom, 0.0)
             for l in range(degrees)], axis=1).astype(jnp.bfloat16)
        both = jnp.dot(spread, green_2[...], preferred_element_type=jnp.float32)
        return both[:, 0:width] + both[:, width:]

    def solve_own(mom):
        mom_h, mom_l = split2(mom)
        both = solve(jnp.concatenate([mom_h.astype(jnp.float32), mom_l.astype(jnp.float32)], axis=0))
        return both[0:lmp] + both[lmp:]

    for t in range(own):
        make_rows(t, me)
    partial = [add_batch(t, me) for t in range(own)]
    solved = []
    for t in range(own):
        partial[t] = accumulate(half - 1, functools.partial(take_batch, t), partial[t])
        mom_v[t] = partial[t].astype(jnp.bfloat16)
        mom_copy(t).start()
        if t + 1 < own:
            repeat(half - 1, lambda i: make_rows(t + 1, peer(i + 1)))
        solved.append(solve_own(partial[t]))

    share = out_ref.shape[0]
    cells = LANES // FINE
    cell_ids = lax.broadcasted_iota(jnp.int32, (FINE, slots), 0)

    def find_spots(k):
        group = atom_at(k)
        if k > 0:
            pts_copy(ma, group).wait_recv()
        at = rpts[group] - ma * (share * LANES)
        block = at >> (LANES.bit_length() - 1)
        inside = (block >= 0) & (block < share)
        cell = (at >> (FINE.bit_length() - 1)) & (cells - 1)
        spot_v[group] = jnp.where(inside, cell * share + block, -1)
        rpts[group] = at & (FINE - 1)

        def mark(a):
            column = rpts[group, pl.ds(a, 1), :]
            onehot[group, a] = jnp.where(cell_ids == column, 1.0, 0.0).astype(jnp.bfloat16)

        repeat(atoms, mark)

    for k in range(n_atom):
        find_spots(k)

    for t in range(own):
        mom_copy(t).wait_recv()
        table = (solved[t] + solve(rmom[t].astype(jnp.float32))).astype(jnp.bfloat16)

        def evaluate(b):
            radial = jnp.dot(table, rows_v[t, b], preferred_element_type=jnp.float32)
            val_v[b, t] = jnp.sum(rang[t, b].astype(jnp.float32) * radial, axis=0, keepdims=True)

        repeat(half - 1, lambda i: evaluate(far_first(i)))
        evaluate(me)
    repeat(half - 1, lambda i: val_copy(far_first(i), ma, me, ma).start())
    for k in range(1, n_atom):
        repeat(half, lambda i: val_copy(peer(half - 1 - i), atom_at(k), me, ma).start())
    rval[ma, me] = val_v[me]

    spot_ids = lax.broadcasted_iota(jnp.int32, (cells * share, slots), 0)

    def add_group(k, terms):
        group = atom_at(k)
        if k == 0:
            repeat(half - 1, lambda i: val_copy(me, ma, peer(i + 1), ma).wait_recv())
        else:
            repeat(half, lambda i: val_copy(me, ma, peer(i), group).wait_recv())

        def placed(a):
            here = spot_ids == spot_v[group, pl.ds(a, 1), :]
            value_h, value_l = split2(rval[group, a // own, a % own])
            spots = jnp.concatenate(
                [jnp.where(here, value_h.astype(jnp.float32), 0.0),
                 jnp.where(here, value_l.astype(jnp.float32), 0.0)], axis=0).astype(jnp.bfloat16)
            return lax.dot_general(spots, onehot[group, a], NT, preferred_element_type=jnp.float32)

        return accumulate(atoms, placed, terms)

    terms = jnp.zeros((2 * cells * share, FINE), jnp.float32)
    for k in range(n_atom):
        terms = add_group(k, terms)
    terms = terms[0:cells * share] + terms[cells * share:]
    out_ref[...] = jnp.concatenate(
        [terms[c * share:(c + 1) * share] for c in range(cells)], axis=1)

    def finish(i):
        to = peer(i + 1)
        for t in range(own):
            ang_copy(t, to, me).wait_send()
        meta_copy(to, me).wait_send()
        val_copy(to, ma, me, ma).wait_send()

    repeat(half - 1, finish)
    for t in range(own):
        mom_copy(t).wait_send()
    for k in range(1, n_atom):
        pts_copy(atom_at(k), ma).wait_send()
        repeat(half, lambda i: val_copy(peer(i), atom_at(k), me, ma).wait_send())


def solution(mesh):
    n_shell, n_atom = mesh.shape["shell"], mesh.shape["atom"]

    def per_device(rho, task_point, task_count, radial_index, fraction, angular, green):
        _, atoms, lm, slots = angular.shape
        points = rho.shape[0]
        degrees, width, _ = green.shape
        half = n_shell // 2
        own = atoms // half
        assert n_shell % 2 == 0 and atoms == half * own and points % (LANES * n_atom) == 0
        assert degrees == math.isqrt(lm)
        coarse = points // LANES
        share = coarse // n_atom
        lmp = (lm // 16 + 1) * 16
        meta_rows = 3 + lm % 16
        f32, bf16, i32 = jnp.float32, jnp.bfloat16, jnp.int32
        vmem = pltpu.VMEM
        scratch = [
            vmem((coarse, LANES), f32),
            vmem((atoms, slots), i32),
            vmem((1, atoms), i32),
            vmem((atoms, slots), i32),
            vmem((atoms, slots), f32),
            vmem((lm, atoms, slots), bf16),
            vmem((slots // LANES, lm * atoms, LANES), f32),
            vmem((atoms, lm // 16 * 16, slots), bf16),
            vmem((degrees, width, width), f32),
            vmem((atoms, slots), f32),
            vmem((atoms, slots), i32),
            vmem((atoms, slots), i32),
            vmem((n_atom, atoms, slots), i32),
            vmem((n_atom, atoms, slots), i32),
            vmem((n_atom, atoms, FINE, slots), bf16),
            vmem((half, own, meta_rows, slots), f32),
            vmem((half, own, meta_rows, slots), f32),
            vmem((own, half, lmp, slots), bf16),
            vmem((own, half, width, slots), bf16),
            vmem((degrees * width, 2 * width), bf16),
            vmem((own, lmp, width), bf16),
            vmem((own, lmp, width), bf16),
            vmem((half, own, 1, slots), f32),
            vmem((n_atom, half, own, 1, slots), f32),
        ] + [pltpu.SemaphoreType.DMA(shape) for shape in (
            (6 + PIECES,), (own, half), (own, half), (half,), (half,), (own,), (own,), (n_atom, half),
            (n_atom, half), (n_atom,), (n_atom,))]
        out = pl.pallas_call(
            functools.partial(kernel, n_shell, n_atom),
            out_shape=pltpu.VMEM((share, LANES), f32),
            in_specs=[pl.BlockSpec(memory_space=pltpu.HBM)] * 7,
            out_specs=pl.BlockSpec(memory_space=pltpu.VMEM),
            scratch_shapes=scratch,
            compiler_params=pltpu.CompilerParams(
                collective_id=0, has_side_effects=True, vmem_limit_bytes=48 * 1024 * 1024),
            name="hartree",
        )(*[pltpu.with_memory_space_constraint(x, pltpu.HBM) for x in (
            rho.reshape(coarse, LANES), task_point, task_count, radial_index, fraction,
            jnp.transpose(angular, (0, 2, 1, 3)), green)])
        return out.reshape(share * LANES)

    in_specs = (
        P("shell"),
        P("shell", "atom", None),
        P("shell", "atom"),
        P("shell", "atom", None),
        P("shell", "atom", None),
        P("shell", "atom", None, None),
        P(),
    )
    return jax.shard_map(
        per_device, mesh=mesh, in_specs=in_specs, out_specs=P(("shell", "atom")), check_vma=False
    )
```

```python
import functools
import math

import jax
import jax.numpy as jnp
from jax import lax
from jax.experimental import pallas as pl
from jax.experimental.pallas import tpu as pltpu
from jax.sharding import PartitionSpec as P

MESH = pl.DeviceIdType.MESH
LANES = 128
FINE = 64
PIECES = 1
NT = (((1,), (1,)), ((), ()))


def repeat(count, body):
    if count <= 16:
        for i in range(count):
            body(i)
    else:
        lax.fori_loop(0, count, lambda i, c: (body(i), c)[1], 0)


def accumulate(count, body, total):
    if count <= 16:
        for i in range(count):
            total = total + body(i)
        return total
    return lax.fori_loop(0, count, lambda i, c: c + body(i), total)


def split2(x):
    high = x.astype(jnp.bfloat16)
    low = (x - high.astype(jnp.float32)).astype(jnp.bfloat16)
    return high, low


def kernel(n_shell, n_atom, rho_h, pts_h, cnt_h, idx_h, frac_h, ang_h, green_h, out_ref,
           rho_v, pts_v, cnt_v, idx_v, frac_v, ang_s, ang_f, ang_v, green_v,
           live_v, low_v, high_v, rpts, spot_v, onehot, meta_v, rmeta, rang, rows_v, green_2,
           mom_v, rmom, val_v, rval,
           local_sem, s_ang, r_ang, s_meta, r_meta, s_mom, r_mom, s_val, r_val, s_pts, r_pts):
    shell, ma = lax.axis_index("shell"), lax.axis_index("atom")
    half, own = val_v.shape[0], val_v.shape[1]
    me = lax.rem(shell, half)
    base = shell - me
    mirror = lax.rem(shell + half, n_shell)
    lm, atoms, slots = ang_s.shape
    lmp = rang.shape[2]
    body_rows = ang_v.shape[1]
    rest = lm - body_rows
    halves = slots // LANES
    degrees, width = green_v.shape[0], green_v.shape[1]
    coarse = rho_v.shape[0]

    def load(i, src, dst):
        copy = pltpu.make_async_copy(src, dst, local_sem.at[i])
        copy.start()
        return copy

    bounds = [lm * i // PIECES for i in range(PIECES + 1)]
    c_ang = [load(6 + i, ang_h.at[0, pl.ds(low, high - low)], ang_s.at[pl.ds(low, high - low)])
             for i, (low, high) in enumerate(zip(bounds, bounds[1:]))]
    c_pts = load(0, pts_h.at[0], pts_v)
    c_rho = load(1, rho_h, rho_v)
    c_idx = load(2, idx_h.at[0], idx_v)
    c_cnt = load(3, cnt_h, cnt_v)
    c_frac = load(4, frac_h.at[0], frac_v)

    def peer(k):
        return lax.rem(me + k, half)

    def atom_at(k):
        return lax.rem(ma + k, n_atom)

    def far_first(i):
        step = (i + 1) // 2
        return peer(half // 2 + step * (1 - 2 * (i % 2)))

    barrier = pltpu.get_barrier_semaphore()
    repeat(half - 1, lambda i: pl.semaphore_signal(
        barrier, inc=1, device_id=(base + peer(i + 1), ma), device_id_type=MESH))
    pl.semaphore_signal(barrier, inc=1, device_id=(mirror, ma), device_id_type=MESH)
    repeat(n_atom - 1, lambda i: pl.semaphore_signal(
        barrier, inc=1, device_id=(shell, atom_at(i + 1)), device_id_type=MESH))
    c_green = load(5, green_h, green_v)

    def ang_copy(t, to, slot):
        return pltpu.make_async_remote_copy(
            src_ref=ang_v.at[to * own + t], dst_ref=rang.at[t, slot, pl.ds(0, body_rows)],
            send_sem=s_ang.at[t, to], recv_sem=r_ang.at[t, slot],
            device_id=(base + to, ma), device_id_type=MESH)

    def meta_copy(to, slot):
        return pltpu.make_async_remote_copy(
            src_ref=meta_v.at[to], dst_ref=rmeta.at[slot],
            send_sem=s_meta.at[to], recv_sem=r_meta.at[slot],
            device_id=(base + to, ma), device_id_type=MESH)

    def mom_copy(t):
        return pltpu.make_async_remote_copy(
            src_ref=mom_v.at[t], dst_ref=rmom.at[t],
            send_sem=s_mom.at[t], recv_sem=r_mom.at[t],
            device_id=(mirror, ma), device_id_type=MESH)

    def val_copy(to, group, slot, from_group):
        return pltpu.make_async_remote_copy(
            src_ref=val_v.at[to], dst_ref=rval.at[from_group, slot],
            send_sem=s_val.at[group], recv_sem=r_val.at[from_group],
            device_id=(base + to, group), device_id_type=MESH)

    def pts_copy(group, slot):
        return pltpu.make_async_remote_copy(
            src_ref=pts_v, dst_ref=rpts.at[slot],
            send_sem=s_pts.at[group], recv_sem=r_pts.at[slot],
            device_id=(shell, group), device_id_type=MESH)

    def widen(m):
        at = pl.multiple_of(m * atoms, 8) if atoms % 8 == 0 else m * atoms
        for h in range(halves):
            ang_f[h, pl.ds(at, atoms), :] = ang_s[m, :, h * LANES:(h + 1) * LANES].astype(jnp.float32)

    def by_atom(a):
        for h in range(halves):
            ang_v[a, :, h * LANES:(h + 1) * LANES] = ang_f[
                h, pl.ds(a, body_rows, stride=atoms), :].astype(jnp.bfloat16)

    for copy, low, high in zip(c_ang, bounds, bounds[1:]):
        copy.wait()
        repeat(high - low, lambda i: widen(low + i))
    repeat(atoms, by_atom)
    pl.semaphore_wait(barrier, half + n_atom - 1)
    repeat(half - 1, lambda i: ang_copy(0, far_first(i), me).start())

    c_pts.wait()
    repeat(n_atom - 1, lambda i: pts_copy(atom_at(i + 1), ma).start())
    c_rho.wait()
    c_idx.wait()
    c_cnt.wait()
    c_frac.wait()
    low_v[...] = pts_v[...] & (LANES - 1)
    high_v[...] = pts_v[...] >> (LANES.bit_length() - 1)
    count_row = jnp.broadcast_to(cnt_v[...].astype(jnp.float32), (atoms, atoms))
    diagonal = (lax.broadcasted_iota(jnp.int32, (atoms, atoms), 0)
                == lax.broadcasted_iota(jnp.int32, (atoms, atoms), 1))
    counts = jnp.sum(jnp.where(diagonal, count_row, 0.0), axis=1, keepdims=True)
    slot_ids = lax.broadcasted_iota(jnp.int32, (atoms, slots), 1).astype(jnp.float32)
    live_v[...] = jnp.where(slot_ids < counts, idx_v[...].astype(jnp.float32), -8.0)

    rho = rho_v[...]
    rho_1 = rho.astype(jnp.bfloat16)
    rho_2, rho_3 = split2(rho - rho_1.astype(jnp.float32))
    rho_parts = jnp.concatenate(
        [rho_1.astype(jnp.float32), rho_2.astype(jnp.float32), rho_3.astype(jnp.float32)],
        axis=0).astype(jnp.bfloat16)
    fine_ids = lax.broadcasted_iota(jnp.int32, (LANES, slots), 0)
    coarse_ids = lax.broadcasted_iota(jnp.int32, (coarse, slots), 0)

    def build_meta(a):
        hot = jnp.where(fine_ids == low_v[pl.ds(a, 1), :], 1.0, 0.0).astype(jnp.bfloat16)
        found = jnp.dot(rho_parts, hot, preferred_element_type=jnp.float32)
        found = found[0:coarse] + found[coarse:2 * coarse] + found[2 * coarse:3 * coarse]
        here = coarse_ids == high_v[pl.ds(a, 1), :]
        to, t = a // own, a % own
        meta_v[to, t, 0:1, :] = jnp.sum(jnp.where(here, found, 0.0), axis=0, keepdims=True)
        meta_v[to, t, 1:2, :] = live_v[pl.ds(a, 1), :]
        meta_v[to, t, 2:3, :] = frac_v[pl.ds(a, 1), :]
        for j in range(rest):
            for h in range(halves):
                meta_v[to, t, 3 + j:4 + j, h * LANES:(h + 1) * LANES] = ang_f[
                    h, pl.ds((body_rows + j) * atoms + a, 1), :]

    repeat(atoms, build_meta)
    repeat(half - 1, lambda i: meta_copy(far_first(i), me).start())
    for t in range(1, own):
        repeat(half - 1, lambda i: ang_copy(t, far_first(i), me).start())
    rmeta[me] = meta_v[me]
    rpts[ma] = pts_v[...]
    for t in range(own):
        rang[t, me, 0:body_rows] = ang_v[me * own + t]

    c_green.wait()
    green = green_v[...].reshape(degrees * width, width)
    gh, gl = split2(green)
    green_2[:, 0:width] = gh
    green_2[:, width:2 * width] = gl

    grid_ids = lax.broadcasted_iota(jnp.int32, (width, slots), 0).astype(jnp.float32)
    tail_ids = lax.broadcasted_iota(jnp.int32, (lmp - body_rows, slots), 0)

    def make_rows(t, s):
        index, fraction = rmeta[s, t, 1:2, :], rmeta[s, t, 2:3, :]
        offset = grid_ids - index
        rows = jnp.where(offset == 0.0, 1.0 - fraction, jnp.where(offset == 1.0, fraction, 0.0))
        rows_v[t, s] = rows.astype(jnp.bfloat16)
        tail = jnp.zeros((lmp - body_rows, slots), jnp.float32)
        for j in range(rest):
            tail = jnp.where(tail_ids == j, rmeta[s, t, 3 + j:4 + j, :], tail)
        rang[t, s, body_rows:lmp] = tail.astype(jnp.bfloat16)

    def add_batch(t, s):
        weighted = (rang[t, s].astype(jnp.float32) * rmeta[s, t, 0:1, :]).astype(jnp.bfloat16)
        return lax.dot_general(weighted, rows_v[t, s], NT, preferred_element_type=jnp.float32)

    def take_batch(t, i):
        s = peer(i + 1)
        if t == 0:
            meta_copy(me, s).wait_recv()
            make_rows(t, s)
        ang_copy(t, me, s).wait_recv()
        return add_batch(t, s)

    def solve(mom):
        rows = mom.shape[0]
        ids = lax.broadcasted_iota(jnp.int32, (rows, width), 0)
        ids = jnp.where(ids >= lmp, ids - lmp, ids)
        spread = jnp.concatenate(
            [jnp.where((ids >= l * l) & (ids < (l + 1) * (l + 1)), mom, 0.0)
             for l in range(degrees)], axis=1).astype(jnp.bfloat16)
        both = jnp.dot(spread, green_2[...], preferred_element_type=jnp.float32)
        return both[:, 0:width] + both[:, width:]

    def solve_own(mom):
        mom_h, mom_l = split2(mom)
        both = solve(jnp.concatenate([mom_h.astype(jnp.float32), mom_l.astype(jnp.float32)], axis=0))
        return both[0:lmp] + both[lmp:]

    for t in range(own):
        make_rows(t, me)
    partial = [add_batch(t, me) for t in range(own)]
    for t in range(own):
        partial[t] = accumulate(half - 1, functools.partial(take_batch, t), partial[t])
        mom_v[t] = partial[t].astype(jnp.bfloat16)
        mom_copy(t).start()
        if t + 1 < own:
            repeat(half - 1, lambda i: make_rows(t + 1, peer(i + 1)))

    share = out_ref.shape[0]
    cells = LANES // FINE
    cell_ids = lax.broadcasted_iota(jnp.int32, (FINE, slots), 0)

    def find_spots(k):
        group = atom_at(k)
        if k > 0:
            pts_copy(ma, group).wait_recv()
        at = rpts[group] - ma * (share * LANES)
        block = at >> (LANES.bit_length() - 1)
        inside = (block >= 0) & (block < share)
        cell = (at >> (FINE.bit_length() - 1)) & (cells - 1)
        spot_v[group] = jnp.where(inside, cell * share + block, -1)
        rpts[group] = at & (FINE - 1)

        def mark(a):
            column = rpts[group, pl.ds(a, 1), :]
            onehot[group, a] = jnp.where(cell_ids == column, 1.0, 0.0).astype(jnp.bfloat16)

        repeat(atoms, mark)

    for k in range(n_atom):
        find_spots(k)

    solved = [solve_own(partial[t]) for t in range(own)]

    def sent(i):
        to = peer(i + 1)
        for t in range(own):
            ang_copy(t, to, me).wait_send()
        meta_copy(to, me).wait_send()

    repeat(half - 1, sent)
    repeat(n_atom - 1, lambda i: pts_copy(atom_at(i + 1), ma).wait_send())

    for t in range(own):
        mom_copy(t).wait_recv()
        table = (solved[t] + solve(rmom[t].astype(jnp.float32))).astype(jnp.bfloat16)

        def evaluate(b):
            radial = jnp.dot(table, rows_v[t, b], preferred_element_type=jnp.float32)
            val_v[b, t] = jnp.sum(rang[t, b].astype(jnp.float32) * radial, axis=0, keepdims=True)

        repeat(half - 1, lambda i: evaluate(far_first(i)))
        evaluate(me)
    repeat(half - 1, lambda i: val_copy(far_first(i), ma, me, ma).start())
    for k in range(1, n_atom):
        repeat(half, lambda i: val_copy(peer(half - 1 - i), atom_at(k), me, ma).start())
    rval[ma, me] = val_v[me]

    def val_batch(group, first, count):
        return pltpu.make_async_remote_copy(
            src_ref=val_v.at[pl.ds(first, count)], dst_ref=rval.at[group, pl.ds(first, count)],
            send_sem=s_val.at[group], recv_sem=r_val.at[group],
            device_id=(mirror, ma), device_id_type=MESH)

    spot_ids = lax.broadcasted_iota(jnp.int32, (cells * share, slots), 0)

    def add_group(k, terms):
        group = atom_at(k)
        if k == 0:
            val_batch(ma, 0, half - 1).wait_recv()
        else:
            val_batch(group, 0, half).wait_recv()

        def placed(a):
            here = spot_ids == spot_v[group, pl.ds(a, 1), :]
            value_h, value_l = split2(rval[group, a // own, a % own])
            spots = jnp.concatenate(
                [jnp.where(here, value_h.astype(jnp.float32), 0.0),
                 jnp.where(here, value_l.astype(jnp.float32), 0.0)], axis=0).astype(jnp.bfloat16)
            return lax.dot_general(spots, onehot[group, a], NT, preferred_element_type=jnp.float32)

        return accumulate(atoms, placed, terms)

    terms = jnp.zeros((2 * cells * share, FINE), jnp.float32)
    for k in range(n_atom):
        terms = add_group(k, terms)
    terms = terms[0:cells * share] + terms[cells * share:]
    out_ref[...] = jnp.concatenate(
        [terms[c * share:(c + 1) * share] for c in range(cells)], axis=1)

    val_batch(ma, 0, half - 1).wait_send()
    for k in range(1, n_atom):
        val_batch(atom_at(k), 0, half).wait_send()
    for t in range(own):
        mom_copy(t).wait_send()


def solution(mesh):
    n_shell, n_atom = mesh.shape["shell"], mesh.shape["atom"]

    def per_device(rho, task_point, task_count, radial_index, fraction, angular, green):
        _, atoms, lm, slots = angular.shape
        points = rho.shape[0]
        degrees, width, _ = green.shape
        half = n_shell // 2
        own = atoms // half
        assert n_shell % 2 == 0 and atoms == half * own and points % (LANES * n_atom) == 0
        assert degrees == math.isqrt(lm)
        coarse = points // LANES
        share = coarse // n_atom
        lmp = (lm // 16 + 1) * 16
        meta_rows = 3 + lm % 16
        f32, bf16, i32 = jnp.float32, jnp.bfloat16, jnp.int32
        vmem = pltpu.VMEM
        scratch = [
            vmem((coarse, LANES), f32),
            vmem((atoms, slots), i32),
            vmem((1, atoms), i32),
            vmem((atoms, slots), i32),
            vmem((atoms, slots), f32),
            vmem((lm, atoms, slots), bf16),
            vmem((slots // LANES, lm * atoms, LANES), f32),
            vmem((atoms, lm // 16 * 16, slots), bf16),
            vmem((degrees, width, width), f32),
            vmem((atoms, slots), f32),
            vmem((atoms, slots), i32),
            vmem((atoms, slots), i32),
            vmem((n_atom, atoms, slots), i32),
            vmem((n_atom, atoms, slots), i32),
            vmem((n_atom, atoms, FINE, slots), bf16),
            vmem((half, own, meta_rows, slots), f32),
            vmem((half, own, meta_rows, slots), f32),
            vmem((own, half, lmp, slots), bf16),
            vmem((own, half, width, slots), bf16),
            vmem((degrees * width, 2 * width), bf16),
            vmem((own, lmp, width), bf16),
            vmem((own, lmp, width), bf16),
            vmem((half, own, 1, slots), f32),
            vmem((n_atom, half, own, 1, slots), f32),
        ] + [pltpu.SemaphoreType.DMA(shape) for shape in (
            (6 + PIECES,), (own, half), (own, half), (half,), (half,), (own,), (own,), (n_atom,),
            (n_atom,), (n_atom,), (n_atom,))]
        out = pl.pallas_call(
            functools.partial(kernel, n_shell, n_atom),
            out_shape=pltpu.VMEM((share, LANES), f32),
            in_specs=[pl.BlockSpec(memory_space=pltpu.HBM)] * 7,
            out_specs=pl.BlockSpec(memory_space=pltpu.VMEM),
            scratch_shapes=scratch,
            compiler_params=pltpu.CompilerParams(
                collective_id=0, has_side_effects=True, vmem_limit_bytes=48 * 1024 * 1024),
            name="hartree",
        )(*[pltpu.with_memory_space_constraint(x, pltpu.HBM) for x in (
            rho.reshape(coarse, LANES), task_point, task_count, radial_index, fraction,
            jnp.transpose(angular, (0, 2, 1, 3)), green)])
        return out.reshape(share * LANES)

    in_specs = (
        P("shell"),
        P("shell", "atom", None),
        P("shell", "atom"),
        P("shell", "atom", None),
        P("shell", "atom", None),
        P("shell", "atom", None, None),
        P(),
    )
    return jax.shard_map(
        per_device, mesh=mesh, in_specs=in_specs, out_specs=P(("shell", "atom")), check_vma=False
    )
```

```python
import functools
import math

import jax
import jax.numpy as jnp
from jax import lax
from jax.experimental import pallas as pl
from jax.experimental.pallas import tpu as pltpu
from jax.sharding import PartitionSpec as P

MESH = pl.DeviceIdType.MESH
LANES = 128
FINE = 64
PIECES = 1
NT = (((1,), (1,)), ((), ()))


def repeat(count, body):
    if count <= 16:
        for i in range(count):
            body(i)
    else:
        lax.fori_loop(0, count, lambda i, c: (body(i), c)[1], 0)


def accumulate(count, body, total):
    if count <= 16:
        for i in range(count):
            total = total + body(i)
        return total
    return lax.fori_loop(0, count, lambda i, c: c + body(i), total)


def split2(x):
    high = x.astype(jnp.bfloat16)
    low = (x - high.astype(jnp.float32)).astype(jnp.bfloat16)
    return high, low


def kernel(n_shell, n_atom, rho_h, pts_h, cnt_h, idx_h, frac_h, ang_h, green_h, out_ref,
           rho_v, pts_v, cnt_v, idx_v, frac_v, ang_s, ang_f, ang_v, green_v,
           live_v, low_v, high_v, rpts, spot_v, onehot, meta_v, rmeta, rang, rows_v, green_2,
           mom_v, rmom, val_v, rval,
           local_sem, s_ang, r_ang, s_meta, r_meta, s_mom, r_mom, s_val, r_val, s_pts, r_pts):
    shell, ma = lax.axis_index("shell"), lax.axis_index("atom")
    half, own = val_v.shape[0], val_v.shape[1]
    me = lax.rem(shell, half)
    base = shell - me
    mirror = lax.rem(shell + half, n_shell)
    lm, atoms, slots = ang_s.shape
    lmp = rang.shape[2]
    body_rows = ang_v.shape[1]
    rest = lm - body_rows
    halves = slots // LANES
    degrees, width = green_v.shape[0], green_v.shape[1]
    coarse = rho_v.shape[0]

    def load(i, src, dst):
        copy = pltpu.make_async_copy(src, dst, local_sem.at[i])
        copy.start()
        return copy

    bounds = [lm * i // PIECES for i in range(PIECES + 1)]
    c_ang = [load(6 + i, ang_h.at[0, pl.ds(low, high - low)], ang_s.at[pl.ds(low, high - low)])
             for i, (low, high) in enumerate(zip(bounds, bounds[1:]))]

    def peer(k):
        return lax.rem(me + k, half)

    def atom_at(k):
        return lax.rem(ma + k, n_atom)

    def far_first(i):
        step = (i + 1) // 2
        return peer(half // 2 + step * (1 - 2 * (i % 2)))

    barrier = pltpu.get_barrier_semaphore()
    repeat(half - 1, lambda i: pl.semaphore_signal(
        barrier, inc=1, device_id=(base + peer(i + 1), ma), device_id_type=MESH))
    pl.semaphore_signal(barrier, inc=1, device_id=(mirror, ma), device_id_type=MESH)
    repeat(n_atom - 1, lambda i: pl.semaphore_signal(
        barrier, inc=1, device_id=(shell, atom_at(i + 1)), device_id_type=MESH))
    c_pts = load(0, pts_h.at[0], pts_v)
    c_rho = load(1, rho_h, rho_v)
    c_idx = load(2, idx_h.at[0], idx_v)
    c_cnt = load(3, cnt_h, cnt_v)
    c_frac = load(4, frac_h.at[0], frac_v)
    c_green = load(5, green_h, green_v)

    def ang_copy(t, to, slot):
        return pltpu.make_async_remote_copy(
            src_ref=ang_v.at[to * own + t], dst_ref=rang.at[t, slot, pl.ds(0, body_rows)],
            send_sem=s_ang.at[t, to], recv_sem=r_ang.at[t, slot],
            device_id=(base + to, ma), device_id_type=MESH)

    def meta_copy(to, slot):
        return pltpu.make_async_remote_copy(
            src_ref=meta_v.at[to], dst_ref=rmeta.at[slot],
            send_sem=s_meta.at[to], recv_sem=r_meta.at[slot],
            device_id=(base + to, ma), device_id_type=MESH)

    def mom_copy(t):
        return pltpu.make_async_remote_copy(
            src_ref=mom_v.at[t], dst_ref=rmom.at[t],
            send_sem=s_mom.at[t], recv_sem=r_mom.at[t],
            device_id=(mirror, ma), device_id_type=MESH)

    def val_copy(to, group, slot, from_group):
        return pltpu.make_async_remote_copy(
            src_ref=val_v.at[to], dst_ref=rval.at[from_group, slot],
            send_sem=s_val.at[group], recv_sem=r_val.at[from_group],
            device_id=(base + to, group), device_id_type=MESH)

    def pts_copy(group, slot):
        return pltpu.make_async_remote_copy(
            src_ref=pts_v, dst_ref=rpts.at[slot],
            send_sem=s_pts.at[group], recv_sem=r_pts.at[slot],
            device_id=(shell, group), device_id_type=MESH)

    def widen(m):
        at = pl.multiple_of(m * atoms, 8) if atoms % 8 == 0 else m * atoms
        for h in range(halves):
            ang_f[h, pl.ds(at, atoms), :] = ang_s[m, :, h * LANES:(h + 1) * LANES].astype(jnp.float32)

    def by_atom(a):
        for h in range(halves):
            ang_v[a, :, h * LANES:(h + 1) * LANES] = ang_f[
                h, pl.ds(a, body_rows, stride=atoms), :].astype(jnp.bfloat16)

    for copy, low, high in zip(c_ang, bounds, bounds[1:]):
        copy.wait()
        repeat(high - low, lambda i: widen(low + i))
    repeat(half, lambda i: by_atom(i * own))
    pl.semaphore_wait(barrier, half + n_atom - 1)
    repeat(half - 1, lambda i: ang_copy(0, far_first(i), me).start())

    c_pts.wait()
    c_rho.wait()
    c_idx.wait()
    c_cnt.wait()
    c_frac.wait()
    low_v[...] = pts_v[...] & (LANES - 1)
    high_v[...] = pts_v[...] >> (LANES.bit_length() - 1)
    count_row = jnp.broadcast_to(cnt_v[...].astype(jnp.float32), (atoms, atoms))
    diagonal = (lax.broadcasted_iota(jnp.int32, (atoms, atoms), 0)
                == lax.broadcasted_iota(jnp.int32, (atoms, atoms), 1))
    counts = jnp.sum(jnp.where(diagonal, count_row, 0.0), axis=1, keepdims=True)
    slot_ids = lax.broadcasted_iota(jnp.int32, (atoms, slots), 1).astype(jnp.float32)
    live_v[...] = jnp.where(slot_ids < counts, idx_v[...].astype(jnp.float32), -8.0)

    rho = rho_v[...]
    rho_1 = rho.astype(jnp.bfloat16)
    rho_2, rho_3 = split2(rho - rho_1.astype(jnp.float32))
    rho_parts = jnp.concatenate(
        [rho_1.astype(jnp.float32), rho_2.astype(jnp.float32), rho_3.astype(jnp.float32)],
        axis=0).astype(jnp.bfloat16)
    fine_ids = lax.broadcasted_iota(jnp.int32, (LANES, slots), 0)
    coarse_ids = lax.broadcasted_iota(jnp.int32, (coarse, slots), 0)

    def build_meta(a):
        hot = jnp.where(fine_ids == low_v[pl.ds(a, 1), :], 1.0, 0.0).astype(jnp.bfloat16)
        found = jnp.dot(rho_parts, hot, preferred_element_type=jnp.float32)
        found = found[0:coarse] + found[coarse:2 * coarse] + found[2 * coarse:3 * coarse]
        here = coarse_ids == high_v[pl.ds(a, 1), :]
        to, t = a // own, a % own
        meta_v[to, t, 0:1, :] = jnp.sum(jnp.where(here, found, 0.0), axis=0, keepdims=True)
        meta_v[to, t, 1:2, :] = live_v[pl.ds(a, 1), :]
        meta_v[to, t, 2:3, :] = frac_v[pl.ds(a, 1), :]
        for j in range(rest):
            for h in range(halves):
                meta_v[to, t, 3 + j:4 + j, h * LANES:(h + 1) * LANES] = ang_f[
                    h, pl.ds((body_rows + j) * atoms + a, 1), :]

    repeat(atoms, build_meta)
    repeat(half - 1, lambda i: meta_copy(far_first(i), me).start())
    for t in range(1, own):
        repeat(half, lambda i: by_atom(i * own + t))
        repeat(half - 1, lambda i: ang_copy(t, far_first(i), me).start())
    repeat(n_atom - 1, lambda i: pts_copy(atom_at(i + 1), ma).start())
    rmeta[me] = meta_v[me]
    rpts[ma] = pts_v[...]
    for t in range(own):
        rang[t, me, 0:body_rows] = ang_v[me * own + t]

    c_green.wait()
    green = green_v[...].reshape(degrees * width, width)
    gh, gl = split2(green)
    green_2[:, 0:width] = gh
    green_2[:, width:2 * width] = gl

    grid_ids = lax.broadcasted_iota(jnp.int32, (width, slots), 0).astype(jnp.float32)
    tail_ids = lax.broadcasted_iota(jnp.int32, (lmp - body_rows, slots), 0)

    def make_rows(t, s):
        index, fraction = rmeta[s, t, 1:2, :], rmeta[s, t, 2:3, :]
        offset = grid_ids - index
        rows = jnp.where(offset == 0.0, 1.0 - fraction, jnp.where(offset == 1.0, fraction, 0.0))
        rows_v[t, s] = rows.astype(jnp.bfloat16)
        tail = jnp.zeros((lmp - body_rows, slots), jnp.float32)
        for j in range(rest):
            tail = jnp.where(tail_ids == j, rmeta[s, t, 3 + j:4 + j, :], tail)
        rang[t, s, body_rows:lmp] = tail.astype(jnp.bfloat16)

    def add_batch(t, s):
        weighted = (rang[t, s].astype(jnp.float32) * rmeta[s, t, 0:1, :]).astype(jnp.bfloat16)
        return lax.dot_general(weighted, rows_v[t, s], NT, preferred_element_type=jnp.float32)

    def take_batch(t, i):
        s = peer(i + 1)
        if t == 0:
            meta_copy(me, s).wait_recv()
            make_rows(t, s)
        ang_copy(t, me, s).wait_recv()
        return add_batch(t, s)

    def solve(mom):
        rows = mom.shape[0]
        ids = lax.broadcasted_iota(jnp.int32, (rows, width), 0)
        ids = jnp.where(ids >= lmp, ids - lmp, ids)
        spread = jnp.concatenate(
            [jnp.where((ids >= l * l) & (ids < (l + 1) * (l + 1)), mom, 0.0)
             for l in range(degrees)], axis=1).astype(jnp.bfloat16)
        both = jnp.dot(spread, green_2[...], preferred_element_type=jnp.float32)
        return both[:, 0:width] + both[:, width:]

    def solve_own(mom):
        mom_h, mom_l = split2(mom)
        both = solve(jnp.concatenate([mom_h.astype(jnp.float32), mom_l.astype(jnp.float32)], axis=0))
        return both[0:lmp] + both[lmp:]

    for t in range(own):
        make_rows(t, me)
    partial = [add_batch(t, me) for t in range(own)]
    for t in range(own):
        partial[t] = accumulate(half - 1, functools.partial(take_batch, t), partial[t])
        mom_v[t] = partial[t].astype(jnp.bfloat16)
        mom_copy(t).start()
        if t + 1 < own:
            repeat(half - 1, lambda i: make_rows(t + 1, peer(i + 1)))

    share = out_ref.shape[0]
    cells = LANES // FINE
    cell_ids = lax.broadcasted_iota(jnp.int32, (FINE, slots), 0)

    def find_spots(k):
        group = atom_at(k)
        if k > 0:
            pts_copy(ma, group).wait_recv()
        at = rpts[group] - ma * (share * LANES)
        block = at >> (LANES.bit_length() - 1)
        inside = (block >= 0) & (block < share)
        cell = (at >> (FINE.bit_length() - 1)) & (cells - 1)
        spot_v[group] = jnp.where(inside, cell * share + block, -1)
        rpts[group] = at & (FINE - 1)

        def mark(a):
            column = rpts[group, pl.ds(a, 1), :]
            onehot[group, a] = jnp.where(cell_ids == column, 1.0, 0.0).astype(jnp.bfloat16)

        repeat(atoms, mark)

    for k in range(n_atom):
        find_spots(k)

    solved = [solve_own(partial[t]) for t in range(own)]

    def sent(i):
        to = peer(i + 1)
        for t in range(own):
            ang_copy(t, to, me).wait_send()
        meta_copy(to, me).wait_send()

    repeat(half - 1, sent)
    repeat(n_atom - 1, lambda i: pts_copy(atom_at(i + 1), ma).wait_send())

    for t in range(own):
        mom_copy(t).wait_recv()
        table = (solved[t] + solve(rmom[t].astype(jnp.float32))).astype(jnp.bfloat16)

        def evaluate(b):
            radial = jnp.dot(table, rows_v[t, b], preferred_element_type=jnp.float32)
            val_v[b, t] = jnp.sum(rang[t, b].astype(jnp.float32) * radial, axis=0, keepdims=True)

        def finish_batch(b):
            evaluate(b)
            if t == own - 1:
                for k in range(1, n_atom):
                    val_copy(b, atom_at(k), me, ma).start()

        def finish_far(i):
            b = far_first(i)
            finish_batch(b)
            if t == own - 1:
                val_copy(b, ma, me, ma).start()

        repeat(half - 1, finish_far)
        finish_batch(me)
    rval[ma, me] = val_v[me]

    def val_batch(group, first, count):
        return pltpu.make_async_remote_copy(
            src_ref=val_v.at[pl.ds(first, count)], dst_ref=rval.at[group, pl.ds(first, count)],
            send_sem=s_val.at[group], recv_sem=r_val.at[group],
            device_id=(mirror, ma), device_id_type=MESH)

    spot_ids = lax.broadcasted_iota(jnp.int32, (cells * share, slots), 0)

    def add_group(k, terms):
        group = atom_at(k)
        if k == 0:
            val_batch(ma, 0, half - 1).wait_recv()
        else:
            val_batch(group, 0, half).wait_recv()

        def placed(a):
            here = spot_ids == spot_v[group, pl.ds(a, 1), :]
            value_h, value_l = split2(rval[group, a // own, a % own])
            spots = jnp.concatenate(
                [jnp.where(here, value_h.astype(jnp.float32), 0.0),
                 jnp.where(here, value_l.astype(jnp.float32), 0.0)], axis=0).astype(jnp.bfloat16)
            return lax.dot_general(spots, onehot[group, a], NT, preferred_element_type=jnp.float32)

        return accumulate(atoms, placed, terms)

    terms = jnp.zeros((2 * cells * share, FINE), jnp.float32)
    for k in range(n_atom):
        terms = add_group(k, terms)
    terms = terms[0:cells * share] + terms[cells * share:]
    out_ref[...] = jnp.concatenate(
        [terms[c * share:(c + 1) * share] for c in range(cells)], axis=1)

    val_batch(ma, 0, half - 1).wait_send()
    for k in range(1, n_atom):
        val_batch(atom_at(k), 0, half).wait_send()
    for t in range(own):
        mom_copy(t).wait_send()


def solution(mesh):
    n_shell, n_atom = mesh.shape["shell"], mesh.shape["atom"]

    def per_device(rho, task_point, task_count, radial_index, fraction, angular, green):
        _, atoms, lm, slots = angular.shape
        points = rho.shape[0]
        degrees, width, _ = green.shape
        half = n_shell // 2
        own = atoms // half
        assert n_shell % 2 == 0 and atoms == half * own and points % (LANES * n_atom) == 0
        assert degrees == math.isqrt(lm)
        coarse = points // LANES
        share = coarse // n_atom
        lmp = (lm // 16 + 1) * 16
        meta_rows = 3 + lm % 16
        f32, bf16, i32 = jnp.float32, jnp.bfloat16, jnp.int32
        vmem = pltpu.VMEM
        scratch = [
            vmem((coarse, LANES), f32),
            vmem((atoms, slots), i32),
            vmem((1, atoms), i32),
            vmem((atoms, slots), i32),
            vmem((atoms, slots), f32),
            vmem((lm, atoms, slots), bf16),
            vmem((slots // LANES, lm * atoms, LANES), f32),
            vmem((atoms, lm // 16 * 16, slots), bf16),
            vmem((degrees, width, width), f32),
            vmem((atoms, slots), f32),
            vmem((atoms, slots), i32),
            vmem((atoms, slots), i32),
            vmem((n_atom, atoms, slots), i32),
            vmem((n_atom, atoms, slots), i32),
            vmem((n_atom, atoms, FINE, slots), bf16),
            vmem((half, own, meta_rows, slots), f32),
            vmem((half, own, meta_rows, slots), f32),
            vmem((own, half, lmp, slots), bf16),
            vmem((own, half, width, slots), bf16),
            vmem((degrees * width, 2 * width), bf16),
            vmem((own, lmp, width), bf16),
            vmem((own, lmp, width), bf16),
            vmem((half, own, 1, slots), f32),
            vmem((n_atom, half, own, 1, slots), f32),
        ] + [pltpu.SemaphoreType.DMA(shape) for shape in (
            (6 + PIECES,), (own, half), (own, half), (half,), (half,), (own,), (own,), (n_atom,),
            (n_atom,), (n_atom,), (n_atom,))]
        out = pl.pallas_call(
            functools.partial(kernel, n_shell, n_atom),
            out_shape=pltpu.VMEM((share, LANES), f32),
            in_specs=[pl.BlockSpec(memory_space=pltpu.HBM)] * 7,
            out_specs=pl.BlockSpec(memory_space=pltpu.VMEM),
            scratch_shapes=scratch,
            compiler_params=pltpu.CompilerParams(
                collective_id=0, has_side_effects=True, vmem_limit_bytes=48 * 1024 * 1024),
            name="hartree",
        )(*[pltpu.with_memory_space_constraint(x, pltpu.HBM) for x in (
            rho.reshape(coarse, LANES), task_point, task_count, radial_index, fraction,
            jnp.transpose(angular, (0, 2, 1, 3)), green)])
        return out.reshape(share * LANES)

    in_specs = (
        P("shell"),
        P("shell", "atom", None),
        P("shell", "atom"),
        P("shell", "atom", None),
        P("shell", "atom", None),
        P("shell", "atom", None, None),
        P(),
    )
    return jax.shard_map(
        per_device, mesh=mesh, in_specs=in_specs, out_specs=P(("shell", "atom")), check_vma=False
    )
```

```python
import functools
import math

import jax
import jax.numpy as jnp
from jax import lax
from jax.experimental import pallas as pl
from jax.experimental.pallas import tpu as pltpu
from jax.sharding import PartitionSpec as P

MESH = pl.DeviceIdType.MESH
LANES = 128
FINE = 64
PIECES = 1
NT = (((1,), (1,)), ((), ()))


def repeat(count, body):
    if count <= 16:
        for i in range(count):
            body(i)
    else:
        lax.fori_loop(0, count, lambda i, c: (body(i), c)[1], 0)


def accumulate(count, body, total):
    if count <= 16:
        for i in range(count):
            total = total + body(i)
        return total
    return lax.fori_loop(0, count, lambda i, c: c + body(i), total)


def split2(x):
    high = x.astype(jnp.bfloat16)
    low = (x - high.astype(jnp.float32)).astype(jnp.bfloat16)
    return high, low


def kernel(n_shell, n_atom, rho_h, pts_h, cnt_h, idx_h, frac_h, ang_h, green_h, out_ref,
           rho_v, pts_v, cnt_v, idx_v, frac_v, ang_s, ang_f, ang_v, green_v,
           live_v, low_v, high_v, rpts, spot_v, onehot, meta_v, rmeta, rang, rows_v, green_2,
           mom_v, rmom, val_v, rval,
           local_sem, s_ang, r_ang, s_meta, r_meta, s_mom, r_mom, s_val, r_val, s_pts, r_pts):
    shell, ma = lax.axis_index("shell"), lax.axis_index("atom")
    half, own = val_v.shape[0], val_v.shape[1]
    me = lax.rem(shell, half)
    base = shell - me
    mirror = lax.rem(shell + half, n_shell)
    lm, atoms, slots = ang_s.shape
    lmp = rang.shape[2]
    body_rows = ang_v.shape[1]
    rest = lm - body_rows
    halves = slots // LANES
    degrees, width = green_v.shape[0], green_v.shape[1]
    coarse = rho_v.shape[0]

    def load(i, src, dst):
        copy = pltpu.make_async_copy(src, dst, local_sem.at[i])
        copy.start()
        return copy

    c_pts = load(0, pts_h.at[0], pts_v)
    c_rho = load(1, rho_h, rho_v)
    c_idx = load(2, idx_h.at[0], idx_v)
    c_cnt = load(3, cnt_h, cnt_v)
    c_frac = load(4, frac_h.at[0], frac_v)
    bounds = [lm * i // PIECES for i in range(PIECES + 1)]
    c_ang = [load(6 + i, ang_h.at[0, pl.ds(low, high - low)], ang_s.at[pl.ds(low, high - low)])
             for i, (low, high) in enumerate(zip(bounds, bounds[1:]))]

    def peer(k):
        return lax.rem(me + k, half)

    def atom_at(k):
        return lax.rem(ma + k, n_atom)

    def far_first(i):
        step = (i + 1) // 2
        return peer(half // 2 + step * (1 - 2 * (i % 2)))

    barrier = pltpu.get_barrier_semaphore()
    repeat(half - 1, lambda i: pl.semaphore_signal(
        barrier, inc=1, device_id=(base + peer(i + 1), ma), device_id_type=MESH))
    pl.semaphore_signal(barrier, inc=1, device_id=(mirror, ma), device_id_type=MESH)
    repeat(n_atom - 1, lambda i: pl.semaphore_signal(
        barrier, inc=1, device_id=(shell, atom_at(i + 1)), device_id_type=MESH))
    c_green = load(5, green_h, green_v)

    def ang_copy(t, to, slot):
        return pltpu.make_async_remote_copy(
            src_ref=ang_v.at[to * own + t], dst_ref=rang.at[t, slot, pl.ds(0, body_rows)],
            send_sem=s_ang.at[t, to], recv_sem=r_ang.at[t, slot],
            device_id=(base + to, ma), device_id_type=MESH)

    def meta_copy(to, slot):
        return pltpu.make_async_remote_copy(
            src_ref=meta_v.at[to], dst_ref=rmeta.at[slot],
            send_sem=s_meta.at[to], recv_sem=r_meta.at[slot],
            device_id=(base + to, ma), device_id_type=MESH)

    def mom_copy(t):
        return pltpu.make_async_remote_copy(
            src_ref=mom_v.at[t], dst_ref=rmom.at[t],
            send_sem=s_mom.at[t], recv_sem=r_mom.at[t],
            device_id=(mirror, ma), device_id_type=MESH)

    def val_copy(to, group, slot, from_group):
        return pltpu.make_async_remote_copy(
            src_ref=val_v.at[to], dst_ref=rval.at[from_group, slot],
            send_sem=s_val.at[group], recv_sem=r_val.at[from_group],
            device_id=(base + to, group), device_id_type=MESH)

    def pts_copy(group, slot):
        return pltpu.make_async_remote_copy(
            src_ref=pts_v, dst_ref=rpts.at[slot],
            send_sem=s_pts.at[group], recv_sem=r_pts.at[slot],
            device_id=(shell, group), device_id_type=MESH)

    c_pts.wait()
    c_rho.wait()
    c_idx.wait()
    c_cnt.wait()
    c_frac.wait()
    low_v[...] = pts_v[...] & (LANES - 1)
    high_v[...] = pts_v[...] >> (LANES.bit_length() - 1)
    count_row = jnp.broadcast_to(cnt_v[...].astype(jnp.float32), (atoms, atoms))
    diagonal = (lax.broadcasted_iota(jnp.int32, (atoms, atoms), 0)
                == lax.broadcasted_iota(jnp.int32, (atoms, atoms), 1))
    counts = jnp.sum(jnp.where(diagonal, count_row, 0.0), axis=1, keepdims=True)
    slot_ids = lax.broadcasted_iota(jnp.int32, (atoms, slots), 1).astype(jnp.float32)
    live_v[...] = jnp.where(slot_ids < counts, idx_v[...].astype(jnp.float32), -8.0)

    rho = rho_v[...]
    rho_1 = rho.astype(jnp.bfloat16)
    rho_2, rho_3 = split2(rho - rho_1.astype(jnp.float32))
    rho_parts = jnp.concatenate(
        [rho_1.astype(jnp.float32), rho_2.astype(jnp.float32), rho_3.astype(jnp.float32)],
        axis=0).astype(jnp.bfloat16)
    fine_ids = lax.broadcasted_iota(jnp.int32, (LANES, slots), 0)
    coarse_ids = lax.broadcasted_iota(jnp.int32, (coarse, slots), 0)

    def build_meta(a):
        hot = jnp.where(fine_ids == low_v[pl.ds(a, 1), :], 1.0, 0.0).astype(jnp.bfloat16)
        found = jnp.dot(rho_parts, hot, preferred_element_type=jnp.float32)
        found = found[0:coarse] + found[coarse:2 * coarse] + found[2 * coarse:3 * coarse]
        here = coarse_ids == high_v[pl.ds(a, 1), :]
        to, t = a // own, a % own
        meta_v[to, t, 0:1, :] = jnp.sum(jnp.where(here, found, 0.0), axis=0, keepdims=True)
        meta_v[to, t, 1:2, :] = live_v[pl.ds(a, 1), :]
        meta_v[to, t, 2:3, :] = frac_v[pl.ds(a, 1), :]
    repeat(atoms, build_meta)

    def widen(m):
        at = pl.multiple_of(m * atoms, 8) if atoms % 8 == 0 else m * atoms
        for h in range(halves):
            ang_f[h, pl.ds(at, atoms), :] = ang_s[m, :, h * LANES:(h + 1) * LANES].astype(jnp.float32)

    def by_atom(a):
        for h in range(halves):
            ang_v[a, :, h * LANES:(h + 1) * LANES] = ang_f[
                h, pl.ds(a, body_rows, stride=atoms), :].astype(jnp.bfloat16)

    for copy, low, high in zip(c_ang, bounds, bounds[1:]):
        copy.wait()
        repeat(high - low, lambda i: widen(low + i))
    repeat(atoms, by_atom)

    def last_rows(a):
        to, t = a // own, a % own
        for j in range(rest):
            for h in range(halves):
                meta_v[to, t, 3 + j:4 + j, h * LANES:(h + 1) * LANES] = ang_f[
                    h, pl.ds((body_rows + j) * atoms + a, 1), :]

    repeat(atoms, last_rows)
    pl.semaphore_wait(barrier, half + n_atom - 1)
    repeat(half - 1, lambda i: meta_copy(far_first(i), me).start())
    for t in range(own):
        repeat(half - 1, lambda i: ang_copy(t, far_first(i), me).start())
    repeat(n_atom - 1, lambda i: pts_copy(atom_at(i + 1), ma).start())
    rmeta[me] = meta_v[me]
    rpts[ma] = pts_v[...]
    for t in range(own):
        rang[t, me, 0:body_rows] = ang_v[me * own + t]

    c_green.wait()
    green = green_v[...].reshape(degrees * width, width)
    gh, gl = split2(green)
    green_2[:, 0:width] = gh
    green_2[:, width:2 * width] = gl

    grid_ids = lax.broadcasted_iota(jnp.int32, (width, slots), 0).astype(jnp.float32)
    tail_ids = lax.broadcasted_iota(jnp.int32, (lmp - body_rows, slots), 0)

    def make_rows(t, s):
        index, fraction = rmeta[s, t, 1:2, :], rmeta[s, t, 2:3, :]
        offset = grid_ids - index
        rows = jnp.where(offset == 0.0, 1.0 - fraction, jnp.where(offset == 1.0, fraction, 0.0))
        rows_v[t, s] = rows.astype(jnp.bfloat16)
        tail = jnp.zeros((lmp - body_rows, slots), jnp.float32)
        for j in range(rest):
            tail = jnp.where(tail_ids == j, rmeta[s, t, 3 + j:4 + j, :], tail)
        rang[t, s, body_rows:lmp] = tail.astype(jnp.bfloat16)

    def add_batch(t, s):
        weighted = (rang[t, s].astype(jnp.float32) * rmeta[s, t, 0:1, :]).astype(jnp.bfloat16)
        return lax.dot_general(weighted, rows_v[t, s], NT, preferred_element_type=jnp.float32)

    def take_batch(t, i):
        s = i + jnp.where(i >= me, 1, 0)
        if t == 0:
            meta_copy(me, s).wait_recv()
        make_rows(t, s)
        ang_copy(t, me, s).wait_recv()
        return add_batch(t, s)

    def solve(mom):
        rows = mom.shape[0]
        ids = lax.broadcasted_iota(jnp.int32, (rows, width), 0)
        ids = jnp.where(ids >= lmp, ids - lmp, ids)
        spread = jnp.concatenate(
            [jnp.where((ids >= l * l) & (ids < (l + 1) * (l + 1)), mom, 0.0)
             for l in range(degrees)], axis=1).astype(jnp.bfloat16)
        both = jnp.dot(spread, green_2[...], preferred_element_type=jnp.float32)
        return both[:, 0:width] + both[:, width:]

    def solve_own(mom):
        mom_h, mom_l = split2(mom)
        both = solve(jnp.concatenate([mom_h.astype(jnp.float32), mom_l.astype(jnp.float32)], axis=0))
        return both[0:lmp] + both[lmp:]

    share = out_ref.shape[0]
    cells = LANES // FINE
    cell_ids = lax.broadcasted_iota(jnp.int32, (FINE, slots), 0)

    def find_spots(k):
        group = atom_at(k)
        if k > 0:
            pts_copy(ma, group).wait_recv()
        at = rpts[group] - ma * (share * LANES)
        block = at >> (LANES.bit_length() - 1)
        inside = (block >= 0) & (block < share)
        cell = (at >> (FINE.bit_length() - 1)) & (cells - 1)
        spot_v[group] = jnp.where(inside, cell * share + block, -1)
        rpts[group] = at & (FINE - 1)

        def mark(a):
            column = rpts[group, pl.ds(a, 1), :]
            onehot[group, a] = jnp.where(cell_ids == column, 1.0, 0.0).astype(jnp.bfloat16)

        repeat(atoms, mark)

    for t in range(own):
        make_rows(t, me)
    partial = [add_batch(t, me) for t in range(own)]
    if half <= 16:
        for i in range(half - 2):
            for t in range(own):
                partial[t] = partial[t] + take_batch(t, i)
    else:
        partial = list(lax.fori_loop(
            0, half - 2, lambda i, c: tuple(c[t] + take_batch(t, i) for t in range(own)), tuple(partial)))
    for t in range(own):
        partial[t] = partial[t] + take_batch(t, half - 2)
        mom_v[t] = partial[t].astype(jnp.bfloat16)
        mom_copy(t).start()

    for k in range(n_atom):
        find_spots(k)

    solved = [solve_own(partial[t]) for t in range(own)]

    for t in range(own):
        mom_copy(t).wait_recv()
        table = (solved[t] + solve(rmom[t].astype(jnp.float32))).astype(jnp.bfloat16)

        def evaluate(b):
            radial = jnp.dot(table, rows_v[t, b], preferred_element_type=jnp.float32)
            val_v[b, t] = jnp.sum(rang[t, b].astype(jnp.float32) * radial, axis=0, keepdims=True)

        def finish_batch(b):
            evaluate(b)
            if t == own - 1:
                for k in range(1, n_atom):
                    val_copy(b, atom_at(k), me, ma).start()

        def finish_far(i):
            b = far_first(i)
            finish_batch(b)
            if t == own - 1:
                val_copy(b, ma, me, ma).start()

        repeat(half - 1, finish_far)
        finish_batch(me)
    rval[ma, me] = val_v[me]

    def sent(i):
        to = peer(i + 1)
        for t in range(own):
            ang_copy(t, to, me).wait_send()
        meta_copy(to, me).wait_send()

    repeat(half - 1, sent)
    repeat(n_atom - 1, lambda i: pts_copy(atom_at(i + 1), ma).wait_send())
    for t in range(own):
        mom_copy(t).wait_send()

    def val_batch(group, first, count):
        return pltpu.make_async_remote_copy(
            src_ref=val_v.at[pl.ds(first, count)], dst_ref=rval.at[group, pl.ds(first, count)],
            send_sem=s_val.at[group], recv_sem=r_val.at[group],
            device_id=(mirror, ma), device_id_type=MESH)

    val_batch(ma, 0, half - 1).wait_send()
    for k in range(1, n_atom):
        val_batch(atom_at(k), 0, half).wait_send()

    spot_ids = lax.broadcasted_iota(jnp.int32, (cells * share, slots), 0)

    def add_group(k, terms):
        group = atom_at(k)
        if k == 0:
            val_batch(ma, 0, half - 1).wait_recv()
        else:
            val_batch(group, 0, half).wait_recv()

        def placed(a):
            here = spot_ids == spot_v[group, pl.ds(a, 1), :]
            value_h, value_l = split2(rval[group, a // own, a % own])
            spots = jnp.concatenate(
                [jnp.where(here, value_h.astype(jnp.float32), 0.0),
                 jnp.where(here, value_l.astype(jnp.float32), 0.0)], axis=0).astype(jnp.bfloat16)
            return lax.dot_general(spots, onehot[group, a], NT, preferred_element_type=jnp.float32)

        return accumulate(atoms, placed, terms)

    terms = jnp.zeros((2 * cells * share, FINE), jnp.float32)
    for k in range(n_atom):
        terms = add_group(k, terms)
    terms = terms[0:cells * share] + terms[cells * share:]
    out_ref[...] = jnp.concatenate(
        [terms[c * share:(c + 1) * share] for c in range(cells)], axis=1)


def solution(mesh):
    n_shell, n_atom = mesh.shape["shell"], mesh.shape["atom"]

    def per_device(rho, task_point, task_count, radial_index, fraction, angular, green):
        _, atoms, lm, slots = angular.shape
        points = rho.shape[0]
        degrees, width, _ = green.shape
        half = n_shell // 2
        own = atoms // half
        assert n_shell % 2 == 0 and atoms == half * own and points % (LANES * n_atom) == 0
        assert degrees == math.isqrt(lm)
        coarse = points // LANES
        share = coarse // n_atom
        lmp = (lm // 16 + 1) * 16
        meta_rows = 3 + lm % 16
        f32, bf16, i32 = jnp.float32, jnp.bfloat16, jnp.int32
        vmem = pltpu.VMEM
        scratch = [
            vmem((coarse, LANES), f32),
            vmem((atoms, slots), i32),
            vmem((1, atoms), i32),
            vmem((atoms, slots), i32),
            vmem((atoms, slots), f32),
            vmem((lm, atoms, slots), bf16),
            vmem((slots // LANES, lm * atoms, LANES), f32),
            vmem((atoms, lm // 16 * 16, slots), bf16),
            vmem((degrees, width, width), f32),
            vmem((atoms, slots), f32),
            vmem((atoms, slots), i32),
            vmem((atoms, slots), i32),
            vmem((n_atom, atoms, slots), i32),
            vmem((n_atom, atoms, slots), i32),
            vmem((n_atom, atoms, FINE, slots), bf16),
            vmem((half, own, meta_rows, slots), f32),
            vmem((half, own, meta_rows, slots), f32),
            vmem((own, half, lmp, slots), bf16),
            vmem((own, half, width, slots), bf16),
            vmem((degrees * width, 2 * width), bf16),
            vmem((own, lmp, width), bf16),
            vmem((own, lmp, width), bf16),
            vmem((half, own, 1, slots), f32),
            vmem((n_atom, half, own, 1, slots), f32),
        ] + [pltpu.SemaphoreType.DMA(shape) for shape in (
            (6 + PIECES,), (own, half), (own, half), (half,), (half,), (own,), (own,), (n_atom,),
            (n_atom,), (n_atom,), (n_atom,))]
        out = pl.pallas_call(
            functools.partial(kernel, n_shell, n_atom),
            out_shape=pltpu.VMEM((share, LANES), f32),
            in_specs=[pl.BlockSpec(memory_space=pltpu.HBM)] * 7,
            out_specs=pl.BlockSpec(memory_space=pltpu.VMEM),
            scratch_shapes=scratch,
            compiler_params=pltpu.CompilerParams(
                collective_id=0, has_side_effects=True, vmem_limit_bytes=48 * 1024 * 1024),
            name="hartree",
        )(*[pltpu.with_memory_space_constraint(x, pltpu.HBM) for x in (
            rho.reshape(coarse, LANES), task_point, task_count, radial_index, fraction,
            jnp.transpose(angular, (0, 2, 1, 3)), green)])
        return out.reshape(share * LANES)

    in_specs = (
        P("shell"),
        P("shell", "atom", None),
        P("shell", "atom"),
        P("shell", "atom", None),
        P("shell", "atom", None),
        P("shell", "atom", None, None),
        P(),
    )
    return jax.shard_map(
        per_device, mesh=mesh, in_specs=in_specs, out_specs=P(("shell", "atom")), check_vma=False
    )
```

```python
import functools
import math

import jax
import jax.numpy as jnp
from jax import lax
from jax.experimental import pallas as pl
from jax.experimental.pallas import tpu as pltpu
from jax.sharding import PartitionSpec as P

MESH = pl.DeviceIdType.MESH
LANES = 128
FINE = 64
PIECES = 1
NT = (((1,), (1,)), ((), ()))


def repeat(count, body):
    if count <= 16:
        for i in range(count):
            body(i)
    else:
        lax.fori_loop(0, count, lambda i, c: (body(i), c)[1], 0)


def accumulate(count, body, total):
    if count <= 16:
        for i in range(count):
            total = total + body(i)
        return total
    return lax.fori_loop(0, count, lambda i, c: c + body(i), total)


def split2(x):
    high = x.astype(jnp.bfloat16)
    low = (x - high.astype(jnp.float32)).astype(jnp.bfloat16)
    return high, low


def kernel(n_shell, n_atom, rho_h, pts_h, cnt_h, idx_h, frac_h, ang_h, green_h, out_ref,
           rho_v, pts_v, cnt_v, idx_v, frac_v, ang_s, ang_f, ang_v, green_v,
           live_v, low_v, high_v, rpts, spot_v, onehot, meta_v, rmeta, rang, rows_v, green_2,
           mom_v, rmom, val_v, rval,
           local_sem, s_ang, r_ang, s_meta, r_meta, s_mom, r_mom, s_val, r_val, s_pts, r_pts):
    shell, ma = lax.axis_index("shell"), lax.axis_index("atom")
    half, own = val_v.shape[0], val_v.shape[1]
    me = lax.rem(shell, half)
    base = shell - me
    mirror = lax.rem(shell + half, n_shell)
    lm, atoms, slots = ang_s.shape
    lmp = rang.shape[2]
    body_rows = ang_v.shape[1]
    rest = lm - body_rows
    halves = slots // LANES
    degrees, width = green_v.shape[0], green_v.shape[1]
    coarse = rho_v.shape[0]

    def load(i, src, dst):
        copy = pltpu.make_async_copy(src, dst, local_sem.at[i])
        copy.start()
        return copy

    bounds = [lm * i // PIECES for i in range(PIECES + 1)]
    c_ang = [load(6 + i, ang_h.at[0, pl.ds(low, high - low)], ang_s.at[pl.ds(low, high - low)])
             for i, (low, high) in enumerate(zip(bounds, bounds[1:]))]

    def peer(k):
        return lax.rem(me + k, half)

    def atom_at(k):
        return lax.rem(ma + k, n_atom)

    def far_first(i):
        step = (i + 1) // 2
        return peer(half // 2 + step * (1 - 2 * (i % 2)))

    barrier = pltpu.get_barrier_semaphore()
    repeat(half - 1, lambda i: pl.semaphore_signal(
        barrier, inc=1, device_id=(base + peer(i + 1), ma), device_id_type=MESH))
    pl.semaphore_signal(barrier, inc=1, device_id=(mirror, ma), device_id_type=MESH)
    repeat(n_atom - 1, lambda i: pl.semaphore_signal(
        barrier, inc=1, device_id=(shell, atom_at(i + 1)), device_id_type=MESH))
    c_pts = load(0, pts_h.at[0], pts_v)
    c_rho = load(1, rho_h, rho_v)
    c_idx = load(2, idx_h.at[0], idx_v)
    c_cnt = load(3, cnt_h, cnt_v)
    c_frac = load(4, frac_h.at[0], frac_v)
    c_green = load(5, green_h, green_v)

    def ang_copy(t, to, slot):
        return pltpu.make_async_remote_copy(
            src_ref=ang_v.at[to * own + t], dst_ref=rang.at[t, slot, pl.ds(0, body_rows)],
            send_sem=s_ang.at[t, to], recv_sem=r_ang.at[t, slot],
            device_id=(base + to, ma), device_id_type=MESH)

    def meta_copy(to, slot):
        return pltpu.make_async_remote_copy(
            src_ref=meta_v.at[to], dst_ref=rmeta.at[slot],
            send_sem=s_meta.at[to], recv_sem=r_meta.at[slot],
            device_id=(base + to, ma), device_id_type=MESH)

    def mom_copy(t):
        return pltpu.make_async_remote_copy(
            src_ref=mom_v.at[t], dst_ref=rmom.at[t],
            send_sem=s_mom.at[t], recv_sem=r_mom.at[t],
            device_id=(mirror, ma), device_id_type=MESH)

    def val_copy(to, group, slot, from_group):
        return pltpu.make_async_remote_copy(
            src_ref=val_v.at[to], dst_ref=rval.at[from_group, slot],
            send_sem=s_val.at[group], recv_sem=r_val.at[from_group],
            device_id=(base + to, group), device_id_type=MESH)

    def pts_copy(group, slot):
        return pltpu.make_async_remote_copy(
            src_ref=pts_v, dst_ref=rpts.at[slot],
            send_sem=s_pts.at[group], recv_sem=r_pts.at[slot],
            device_id=(shell, group), device_id_type=MESH)

    def widen(m):
        at = pl.multiple_of(m * atoms, 8) if atoms % 8 == 0 else m * atoms
        for h in range(halves):
            ang_f[h, pl.ds(at, atoms), :] = ang_s[m, :, h * LANES:(h + 1) * LANES].astype(jnp.float32)

    def by_atom(a):
        for h in range(halves):
            ang_v[a, :, h * LANES:(h + 1) * LANES] = ang_f[
                h, pl.ds(a, body_rows, stride=atoms), :].astype(jnp.bfloat16)

    for copy, low, high in zip(c_ang, bounds, bounds[1:]):
        copy.wait()
        repeat(high - low, lambda i: widen(low + i))
    repeat(half, lambda i: by_atom(i * own))
    pl.semaphore_wait(barrier, half + n_atom - 1)
    repeat(half - 1, lambda i: ang_copy(0, far_first(i), me).start())

    c_pts.wait()
    c_rho.wait()
    c_idx.wait()
    c_cnt.wait()
    c_frac.wait()
    low_v[...] = pts_v[...] & (LANES - 1)
    high_v[...] = pts_v[...] >> (LANES.bit_length() - 1)
    count_row = jnp.broadcast_to(cnt_v[...].astype(jnp.float32), (atoms, atoms))
    diagonal = (lax.broadcasted_iota(jnp.int32, (atoms, atoms), 0)
                == lax.broadcasted_iota(jnp.int32, (atoms, atoms), 1))
    counts = jnp.sum(jnp.where(diagonal, count_row, 0.0), axis=1, keepdims=True)
    slot_ids = lax.broadcasted_iota(jnp.int32, (atoms, slots), 1).astype(jnp.float32)
    live_v[...] = jnp.where(slot_ids < counts, idx_v[...].astype(jnp.float32), -8.0)

    rho = rho_v[...]
    rho_1 = rho.astype(jnp.bfloat16)
    rho_2, rho_3 = split2(rho - rho_1.astype(jnp.float32))
    rho_parts = jnp.concatenate(
        [rho_1.astype(jnp.float32), rho_2.astype(jnp.float32), rho_3.astype(jnp.float32)],
        axis=0).astype(jnp.bfloat16)
    fine_ids = lax.broadcasted_iota(jnp.int32, (LANES, slots), 0)
    coarse_ids = lax.broadcasted_iota(jnp.int32, (coarse, slots), 0)

    def build_meta(a):
        hot = jnp.where(fine_ids == low_v[pl.ds(a, 1), :], 1.0, 0.0).astype(jnp.bfloat16)
        found = jnp.dot(rho_parts, hot, preferred_element_type=jnp.float32)
        found = found[0:coarse] + found[coarse:2 * coarse] + found[2 * coarse:3 * coarse]
        here = coarse_ids == high_v[pl.ds(a, 1), :]
        to, t = a // own, a % own
        meta_v[to, t, 0:1, :] = jnp.sum(jnp.where(here, found, 0.0), axis=0, keepdims=True)
        meta_v[to, t, 1:2, :] = live_v[pl.ds(a, 1), :]
        meta_v[to, t, 2:3, :] = frac_v[pl.ds(a, 1), :]
        for j in range(rest):
            for h in range(halves):
                meta_v[to, t, 3 + j:4 + j, h * LANES:(h + 1) * LANES] = ang_f[
                    h, pl.ds((body_rows + j) * atoms + a, 1), :]

    repeat(atoms, build_meta)
    repeat(half - 1, lambda i: meta_copy(far_first(i), me).start())
    for t in range(1, own):
        repeat(half, lambda i: by_atom(i * own + t))
        repeat(half - 1, lambda i: ang_copy(t, far_first(i), me).start())
    repeat(n_atom - 1, lambda i: pts_copy(atom_at(i + 1), ma).start())
    rmeta[me] = meta_v[me]
    rpts[ma] = pts_v[...]
    for t in range(own):
        rang[t, me, 0:body_rows] = ang_v[me * own + t]

    c_green.wait()
    green = green_v[...].reshape(degrees * width, width)
    gh, gl = split2(green)
    green_2[:, 0:width] = gh
    green_2[:, width:2 * width] = gl

    grid_ids = lax.broadcasted_iota(jnp.int32, (width, slots), 0).astype(jnp.float32)
    tail_ids = lax.broadcasted_iota(jnp.int32, (lmp - body_rows, slots), 0)

    def make_rows(t, s):
        index, fraction = rmeta[s, t, 1:2, :], rmeta[s, t, 2:3, :]
        offset = grid_ids - index
        rows = jnp.where(offset == 0.0, 1.0 - fraction, jnp.where(offset == 1.0, fraction, 0.0))
        rows_v[t, s] = rows.astype(jnp.bfloat16)
        tail = jnp.zeros((lmp - body_rows, slots), jnp.float32)
        for j in range(rest):
            tail = jnp.where(tail_ids == j, rmeta[s, t, 3 + j:4 + j, :], tail)
        rang[t, s, body_rows:lmp] = tail.astype(jnp.bfloat16)

    def add_batch(t, s):
        weighted = (rang[t, s].astype(jnp.float32) * rmeta[s, t, 0:1, :]).astype(jnp.bfloat16)
        return lax.dot_general(weighted, rows_v[t, s], NT, preferred_element_type=jnp.float32)

    def take_batch(t, i):
        s = peer(i + 1)
        if t == 0:
            meta_copy(me, s).wait_recv()
            make_rows(t, s)
        ang_copy(t, me, s).wait_recv()
        return add_batch(t, s)

    def solve(mom):
        rows = mom.shape[0]
        ids = lax.broadcasted_iota(jnp.int32, (rows, width), 0)
        ids = jnp.where(ids >= lmp, ids - lmp, ids)
        spread = jnp.concatenate(
            [jnp.where((ids >= l * l) & (ids < (l + 1) * (l + 1)), mom, 0.0)
             for l in range(degrees)], axis=1).astype(jnp.bfloat16)
        both = jnp.dot(spread, green_2[...], preferred_element_type=jnp.float32)
        return both[:, 0:width] + both[:, width:]

    def solve_own(mom):
        mom_h, mom_l = split2(mom)
        both = solve(jnp.concatenate([mom_h.astype(jnp.float32), mom_l.astype(jnp.float32)], axis=0))
        return both[0:lmp] + both[lmp:]

    share = out_ref.shape[0]
    cells = LANES // FINE
    cell_ids = lax.broadcasted_iota(jnp.int32, (FINE, slots), 0)

    def find_spots(k):
        group = atom_at(k)
        if k > 0:
            pts_copy(ma, group).wait_recv()
        at = rpts[group] - ma * (share * LANES)
        block = at >> (LANES.bit_length() - 1)
        inside = (block >= 0) & (block < share)
        cell = (at >> (FINE.bit_length() - 1)) & (cells - 1)
        spot_v[group] = jnp.where(inside, cell * share + block, -1)
        rpts[group] = at & (FINE - 1)

        def mark(a):
            column = rpts[group, pl.ds(a, 1), :]
            onehot[group, a] = jnp.where(cell_ids == column, 1.0, 0.0).astype(jnp.bfloat16)

        repeat(atoms, mark)

    for t in range(own):
        make_rows(t, me)
    partial = [add_batch(t, me) for t in range(own)]
    for t in range(own):
        partial[t] = accumulate(half - 1, functools.partial(take_batch, t), partial[t])
        mom_v[t] = partial[t].astype(jnp.bfloat16)
        mom_copy(t).start()
        if t + 1 < own:
            repeat(half - 1, lambda i: make_rows(t + 1, peer(i + 1)))

    for k in range(n_atom):
        find_spots(k)

    solved = [solve_own(partial[t]) for t in range(own)]

    for t in range(own):
        mom_copy(t).wait_recv()
        table = (solved[t] + solve(rmom[t].astype(jnp.float32))).astype(jnp.bfloat16)

        def evaluate(b):
            radial = jnp.dot(table, rows_v[t, b], preferred_element_type=jnp.float32)
            val_v[b, t] = jnp.sum(rang[t, b].astype(jnp.float32) * radial, axis=0, keepdims=True)

        def finish_batch(b):
            evaluate(b)
            if t == own - 1:
                for k in range(1, n_atom):
                    val_copy(b, atom_at(k), me, ma).start()

        def finish_far(i):
            b = far_first(i)
            finish_batch(b)
            if t == own - 1:
                val_copy(b, ma, me, ma).start()

        repeat(half - 1, finish_far)
        finish_batch(me)
    rval[ma, me] = val_v[me]

    def sent(i):
        to = peer(i + 1)
        for t in range(own):
            ang_copy(t, to, me).wait_send()
        meta_copy(to, me).wait_send()

    repeat(half - 1, sent)
    repeat(n_atom - 1, lambda i: pts_copy(atom_at(i + 1), ma).wait_send())
    for t in range(own):
        mom_copy(t).wait_send()

    def val_batch(group, first, count):
        return pltpu.make_async_remote_copy(
            src_ref=val_v.at[pl.ds(first, count)], dst_ref=rval.at[group, pl.ds(first, count)],
            send_sem=s_val.at[group], recv_sem=r_val.at[group],
            device_id=(mirror, ma), device_id_type=MESH)

    val_batch(ma, 0, half - 1).wait_send()
    for k in range(1, n_atom):
        val_batch(atom_at(k), 0, half).wait_send()

    spot_ids = lax.broadcasted_iota(jnp.int32, (cells * share, slots), 0)

    def add_group(k, terms):
        group = atom_at(k)
        if k == 0:
            val_batch(ma, 0, half - 1).wait_recv()
        else:
            val_batch(group, 0, half).wait_recv()

        def placed(a):
            here = spot_ids == spot_v[group, pl.ds(a, 1), :]
            value_h, value_l = split2(rval[group, a // own, a % own])
            spots = jnp.concatenate(
                [jnp.where(here, value_h.astype(jnp.float32), 0.0),
                 jnp.where(here, value_l.astype(jnp.float32), 0.0)], axis=0).astype(jnp.bfloat16)
            return lax.dot_general(spots, onehot[group, a], NT, preferred_element_type=jnp.float32)

        return accumulate(atoms, placed, terms)

    terms = jnp.zeros((2 * cells * share, FINE), jnp.float32)
    for k in range(n_atom):
        terms = add_group(k, terms)
    terms = terms[0:cells * share] + terms[cells * share:]
    out_ref[...] = jnp.concatenate(
        [terms[c * share:(c + 1) * share] for c in range(cells)], axis=1)


def solution(mesh):
    n_shell, n_atom = mesh.shape["shell"], mesh.shape["atom"]

    def per_device(rho, task_point, task_count, radial_index, fraction, angular, green):
        _, atoms, lm, slots = angular.shape
        points = rho.shape[0]
        degrees, width, _ = green.shape
        half = n_shell // 2
        own = atoms // half
        assert n_shell % 2 == 0 and atoms == half * own and points % (LANES * n_atom) == 0
        assert degrees == math.isqrt(lm)
        coarse = points // LANES
        share = coarse // n_atom
        lmp = (lm // 16 + 1) * 16
        meta_rows = 3 + lm % 16
        f32, bf16, i32 = jnp.float32, jnp.bfloat16, jnp.int32
        vmem = pltpu.VMEM
        scratch = [
            vmem((coarse, LANES), f32),
            vmem((atoms, slots), i32),
            vmem((1, atoms), i32),
            vmem((atoms, slots), i32),
            vmem((atoms, slots), f32),
            vmem((lm, atoms, slots), bf16),
            vmem((slots // LANES, lm * atoms, LANES), f32),
            vmem((atoms, lm // 16 * 16, slots), bf16),
            vmem((degrees, width, width), f32),
            vmem((atoms, slots), f32),
            vmem((atoms, slots), i32),
            vmem((atoms, slots), i32),
            vmem((n_atom, atoms, slots), i32),
            vmem((n_atom, atoms, slots), i32),
            vmem((n_atom, atoms, FINE, slots), bf16),
            vmem((half, own, meta_rows, slots), f32),
            vmem((half, own, meta_rows, slots), f32),
            vmem((own, half, lmp, slots), bf16),
            vmem((own, half, width, slots), bf16),
            vmem((degrees * width, 2 * width), bf16),
            vmem((own, lmp, width), bf16),
            vmem((own, lmp, width), bf16),
            vmem((half, own, 1, slots), f32),
            vmem((n_atom, half, own, 1, slots), f32),
        ] + [pltpu.SemaphoreType.DMA(shape) for shape in (
            (6 + PIECES,), (own, half), (own, half), (half,), (half,), (own,), (own,), (n_atom,),
            (n_atom,), (n_atom,), (n_atom,))]
        out = pl.pallas_call(
            functools.partial(kernel, n_shell, n_atom),
            out_shape=pltpu.VMEM((share, LANES), f32),
            in_specs=[pl.BlockSpec(memory_space=pltpu.HBM)] * 7,
            out_specs=pl.BlockSpec(memory_space=pltpu.VMEM),
            scratch_shapes=scratch,
            compiler_params=pltpu.CompilerParams(
                collective_id=0, has_side_effects=True, vmem_limit_bytes=48 * 1024 * 1024),
            name="hartree",
        )(*[pltpu.with_memory_space_constraint(x, pltpu.HBM) for x in (
            rho.reshape(coarse, LANES), task_point, task_count, radial_index, fraction,
            jnp.transpose(angular, (0, 2, 1, 3)), green)])
        return out.reshape(share * LANES)

    in_specs = (
        P("shell"),
        P("shell", "atom", None),
        P("shell", "atom"),
        P("shell", "atom", None),
        P("shell", "atom", None),
        P("shell", "atom", None, None),
        P(),
    )
    return jax.shard_map(
        per_device, mesh=mesh, in_specs=in_specs, out_specs=P(("shell", "atom")), check_vma=False
    )
```
